32 devices in a mesh: axial: 8 (over z, y), azim: 4 (over x, core).
Axes of the slice: x: 2, y: 2, z: 4, core: 2. Of those that a mesh axis runs over, the one named last changes fastest.
Arguments:
- tet_state: bfloat16 [175, 32768], P(None, ('axial', 'azim')), may hold values from -6 to 6
- prism_state: bfloat16 [375, 32768], P(None, ('axial', 'azim')), may hold values from -6 to 6
- tet_volume: bfloat16 [175, 175], replicated, may hold values from -0.4375 to 0.4375
- prism_volume: bfloat16 [375, 375], replicated, may hold values from -0.3125 to 0.3125
- face_extrap: bfloat16 [300, 175], replicated, may hold values from -0.4375 to 0.4375
- face_lift: bfloat16 [175, 300], replicated, may hold values from -0.75 to 0.75
- wall_extrap: bfloat16 [75, 375], replicated, may hold values from -0.3125 to 0.3125
- wall_lift: bfloat16 [375, 75], replicated, may hold values from -0.75 to 0.75
- face_code: int32 [32768], P(('axial', 'azim')), may hold values from 0 to 4095, as said below
- face_count: int32 [32, 2], P(('axial', 'azim')), may hold values from 0 to 512, as said below
- face_area: float32 [32768], P(('axial', 'azim')), may hold values from 0.5 to 2
- burn_prism: int32 [16384], P(('axial', 'azim')), may hold values from 0 to 1023, as said below
- burn_owner: int32 [16384, 1], P(('axial', 'azim')), may hold values from 0 to 3; in each aligned block of 512 rows (0 to 511, 512 to 1023, ...) at most 128 rows name the same one
- burn_law: float32 [8, 4, 6], P('axial'), may hold values from 0.5 to 2
Outputs:
- tet_new: bfloat16 [175, 32768], P(None, ('axial', 'azim'))
- prism_new: bfloat16 [375, 32768], P(None, ('axial', 'azim'))
The draws below stay inside these ranges and needn't reach their ends.
Inputs may be any that keep to these rules, and one draw needn't show every extreme that they name: `face_code`: within each partition's block of 1024 entries the codes are distinct; the first 512 are faces shared with the lower axial neighbour, the rest with the upper; upper slot s of (a, z) is the same face as lower slot s of (a+1, z). `face_count`: column 0 counts live lower slots, column 1 live upper slots; the upper count of (a, z) equals the lower count of (a+1, z); zero at the two ends of the axial range, 1 or more elsewhere; 512 is reached. `burn_prism`: distinct within each partition's block. `burn_owner`: at most 128 wall faces of one partition name one owner, and that bound is reached.
All inputs are finite; a program needn't handle non-finite values.
Results may differ from the reference program's by a relative error of at most 0.0043.
Values may be sent and summed in bfloat16 or wider, within the bound.
A program may use at most 64 MiB of HBM per device.

```python
import math
import jax
import jax.numpy as jnp
import numpy as np
from jax import lax

NV = 5
TFP = 15
TW = 175
PW = 375
FW = 75
ET = 1024
EP = 1024
CF = 512
BW_DEV = 512
CB = 128
SLABS = 8
SECTORS = 4
TETS = 32768
PRISMS = 32768


def draw_face_code(key, part):
    subkeys = jax.random.split(key, SLABS * SECTORS)

    def per_device(subkey):
        return jax.random.permutation(subkey, 4 * ET)[:2 * CF].astype(jnp.int32)
    return jax.vmap(per_device)(subkeys).reshape(SLABS * SECTORS * 2 * CF).astype(jnp.int32)


def draw_face_count(key, part):
    key_count, key_pick = jax.random.split(key)
    pairs = jax.random.randint(key_count, (SLABS - 1, SECTORS), 1, CF + 1).astype(jnp.int32)
    flat_pairs = pairs.reshape((SLABS - 1) * SECTORS)
    picked = jax.random.randint(key_pick, (), 0, (SLABS - 1) * SECTORS).astype(jnp.int32)
    flat_pairs = jnp.where(jnp.arange((SLABS - 1) * SECTORS, dtype=jnp.int32) == picked, CF, flat_pairs)
    pairs = flat_pairs.reshape(SLABS - 1, SECTORS)
    zeros_row = jnp.zeros((1, SECTORS), jnp.int32)
    lower = jnp.concatenate([zeros_row, pairs], axis=0)
    upper = jnp.concatenate([pairs, zeros_row], axis=0)
    return jnp.stack([lower, upper], axis=-1).reshape(SLABS * SECTORS, 2).astype(jnp.int32)


def draw_burn_prism(key, part):
    subkeys = jax.random.split(key, SLABS * SECTORS)

    def per_device(subkey):
        return jax.random.permutation(subkey, EP)[:BW_DEV].astype(jnp.int32)
    return jax.vmap(per_device)(subkeys).reshape(SLABS * SECTORS * BW_DEV).astype(jnp.int32)


def block_scale(key, extent, cuts, smallest, high):
    factor_of, own = 1.0, jax.random.fold_in(key, 6)
    for position, parts in cuts:
        steps = jnp.exp(jax.random.uniform(jax.random.fold_in(own, position), (parts,), jnp.float32, smallest / len(cuts), high / len(cuts)))
        factor_of = factor_of * jnp.repeat(steps, extent[position] // parts).reshape([-1 if axis == position else 1 for axis in range(len(extent))])
    return factor_of


def routed_block(stream_key, own, number, rows, number_of, top, reach, slope):
    order = jax.random.permutation(stream_key, number_of)
    heavy_load, common = shares(number_of, rows * top, reach, slope, True), shares(number_of, rows * top, reach, slope, False)
    places = jnp.arange(number_of)

    def named(sizes, turn):
        used = int((sizes > 0).sum())
        fixed = max(1, used // 4)
        passed = fixed + (places - fixed + turn * (used - fixed)) % max(1, number_of - fixed)
        return jnp.zeros((number_of,), jnp.int32).at[order[jnp.where(places < fixed, places, passed)]].set(jnp.asarray(sizes, jnp.int32))

    sizes = jnp.where(number % 4 == 0, named(heavy_load, number // 4), named(common, number - number // 4 - 1))
    mixed = jax.random.permutation(jax.random.fold_in(own, 3), number_of)
    giver, sink = mixed[0:number_of // 2 * 2:2], mixed[1:number_of // 2 * 2:2]
    slack = jnp.minimum(sizes[giver] - 1, reach - sizes[sink]) // 2
    slack = jnp.where((giver == order[0]) | (sink == order[0]) | (sizes[sink] == 0), 0, jnp.maximum(slack, 0))
    passed = jax.random.randint(jax.random.fold_in(own, 4), (number_of // 2,), 0, 1 << 20) % (slack + 1)
    sizes = sizes.at[giver].add(-passed).at[sink].add(passed)
    items = jnp.searchsorted(jnp.cumsum(sizes), jnp.arange(rows * top), side="right").astype(jnp.int32)
    grid = items.reshape(top, rows).T
    grid = grid[jax.random.permutation(jax.random.fold_in(own, 1), rows)]
    turn = jax.random.randint(jax.random.fold_in(own, 2), (rows, 1), 0, top)
    return jnp.take_along_axis(grid, (jnp.arange(top)[None, :] + turn) % top, axis=1)


def shares(count, total, reach, skew, full):
    portions = [(1 << 20) // math.isqrt(grade ** skew) + 1 for grade in range(1, count + 1)]
    largest = reach if full else min(reach, max(-(-total // count), total * portions[0] // sum(portions)))
    least = 1 if total - largest >= count - 1 else 0
    holding, rest = [largest] + [least] * (count - 1), total - largest - least * (count - 1)
    while rest > 0:
        candidates = [i for i in range(1, count) if holding[i] < largest] or [i for i in range(1, count) if holding[i] < reach]
        mass, budget = sum([portions[i] for i in candidates]), rest
        for i in candidates:
            addition = min(reach - holding[i], max(1, budget * portions[i] // mass), rest)
            holding[i] = holding[i] + addition
            rest = rest - addition
    return np.array(holding)


def normal_values(own_key, extent, spread, bound, pieces=(), kind=jnp.bfloat16):
    array = spread * jax.random.normal(own_key, extent, jnp.float32)
    if pieces:
        array = array * block_scale(own_key, extent, pieces, -0.22, 0.18)
    return jnp.clip(array, -bound, bound).astype(kind)


def setup_inputs(seed: int = 0) -> dict:
    keys = jax.random.split(jax.random.key(seed), 15)
    tet_state = normal_values(keys[0], (TW, TETS), 1.0, 6.0, ((1, 32),))
    prism_state = normal_values(keys[1], (PW, PRISMS), 1.0, 6.0, ((1, 32),))
    tet_volume = normal_values(keys[2], (TW, TW), TW ** -0.5, 0.4375)
    prism_volume = normal_values(keys[3], (PW, PW), PW ** -0.5, 0.3125)
    face_extrap = normal_values(keys[4], (4 * FW, TW), TW ** -0.5, 0.4375)
    face_lift = normal_values(keys[5], (TW, 4 * FW), FW ** -0.5, 0.75)
    wall_extrap = normal_values(keys[6], (FW, PW), PW ** -0.5, 0.3125)
    wall_lift = normal_values(keys[7], (PW, FW), FW ** -0.5, 0.75)
    face_code = draw_face_code(jax.random.fold_in(keys[14], 71), 0)
    face_count = draw_face_count(jax.random.fold_in(keys[14], 71), 0)
    face_area = jnp.clip(jnp.exp(math.log(2.0) - 1.3862944 * jax.random.uniform(keys[10], (SLABS * SECTORS * 2 * CF,), jnp.float32) ** block_scale(keys[10], (SLABS * SECTORS * 2 * CF,), ((0, 32),), -0.2, 0.2)), 0.5, 2.0)
    burn_prism = draw_burn_prism(jax.random.fold_in(keys[14], 71), 0)
    burn_owner_keys = jax.random.split(jax.random.fold_in(keys[12], 1), (SLABS * SECTORS * BW_DEV) // BW_DEV)
    burn_owner_turns = jax.random.permutation(jax.random.fold_in(keys[12], 3), (SLABS * SECTORS * BW_DEV) // BW_DEV)
    burn_owner = jax.vmap(lambda own, number: routed_block(jax.random.fold_in(keys[12], 2), own, number, BW_DEV, SECTORS, 1, CB, 2))(burn_owner_keys, burn_owner_turns).reshape((SLABS * SECTORS * BW_DEV, 1))
    burn_law = jnp.clip(0.5 + 1.5 * jax.random.uniform(keys[13], (SLABS, SECTORS, 6), jnp.float32) ** block_scale(keys[13], (SLABS, SECTORS, 6), ((0, 8),), -0.2, 0.2), 0.5, 2.0)
    return {"tet_state": tet_state, "prism_state": prism_state, "tet_volume": tet_volume, "prism_volume": prism_volume, "face_extrap": face_extrap, "face_lift": face_lift, "wall_extrap": wall_extrap, "wall_lift": wall_lift, "face_code": face_code, "face_count": face_count, "face_area": face_area, "burn_prism": burn_prism, "burn_owner": burn_owner, "burn_law": burn_law}


section_step = 0.25


def square_half(values):
    widened = values.astype(jnp.float32)
    return (0.5 * widened * widened).astype(jnp.bfloat16)


def product(left, right):
    return jnp.dot(left.astype(jnp.float32), right.astype(jnp.float32), precision=lax.Precision.HIGHEST, preferred_element_type=jnp.float32)


def reference(tet_state, prism_state, tet_volume, prism_volume, face_extrap, face_lift, wall_extrap, wall_lift, face_code, face_count, face_area, burn_prism, burn_owner, burn_law):
    partitions = SLABS * SECTORS
    slots = 2 * CF
    face_ids = jnp.arange(4, dtype=jnp.int32)

    def left_of(device):
        tet_block = lax.dynamic_slice_in_dim(tet_state, device * ET, ET, 1)
        codes = lax.dynamic_slice_in_dim(face_code, device * slots, slots, 0)
        columns = jnp.take(tet_block, codes // 4, axis=1)
        extended = product(face_extrap, columns).reshape(4, FW, slots)
        chosen = (codes % 4)[None, :] == face_ids[:, None]
        return jnp.sum(jnp.where(chosen[:, None, :], extended, jnp.zeros_like(extended)), axis=0).astype(jnp.bfloat16)

    left_all = lax.map(left_of, jnp.arange(partitions, dtype=jnp.int32))
    face_grid = left_all.reshape(SLABS, SECTORS, FW, 2, CF)
    zeros_row = jnp.zeros((1, SECTORS, FW, CF), jnp.bfloat16)
    from_lower = jnp.concatenate([zeros_row, face_grid[:-1, :, :, 1]], axis=0)
    from_upper = jnp.concatenate([face_grid[1:, :, :, 0], zeros_row], axis=0)
    right_all = jnp.stack([from_lower, from_upper], axis=3).reshape(partitions, FW, slots)

    def wall_of(device):
        prism_block = lax.dynamic_slice_in_dim(prism_state, device * EP, EP, 1)
        prism_index = lax.dynamic_slice_in_dim(burn_prism, device * BW_DEV, BW_DEV, 0)
        columns = jnp.take(prism_block, prism_index, axis=1)
        return product(wall_extrap, columns).astype(jnp.bfloat16)

    wall_all = lax.map(wall_of, jnp.arange(partitions, dtype=jnp.int32))
    pressure = wall_all[:, 4 * TFP:5 * TFP, :].astype(jnp.float32)
    squares = pressure * pressure
    row_sums = jnp.sum(squares, axis=1)
    owners = burn_owner.reshape(partitions, BW_DEV)
    owner_hot = (owners[:, :, None] == jnp.arange(SECTORS, dtype=jnp.int32)[None, None, :]).astype(jnp.float32)
    patch_parts = jnp.einsum("pb,pbs->ps", row_sums, owner_hot, precision=lax.Precision.HIGHEST)
    totals = jnp.sum(patch_parts.reshape(SLABS, SECTORS, SECTORS), axis=1)
    burn_coef = burn_law[:, :, 0]
    damping = 1.0 / (1.0 + burn_coef * totals / (BW_DEV * TFP))
    law_rows = jnp.repeat(burn_law, SECTORS, axis=0)
    damp_rows = jnp.repeat(damping, SECTORS, axis=0)
    coef_each = jnp.sum(owner_hot * law_rows[:, None, :, 0], axis=2)
    damp_each = jnp.sum(owner_hot * damp_rows[:, None, :], axis=2)
    inject_each = jnp.einsum("pbs,psv->pvb", owner_hot, law_rows[:, :, 1:6], precision=lax.Precision.HIGHEST)
    wall_jump = (inject_each[:, :, None, :] * (coef_each * damp_each)[:, None, None, :] * squares[:, None, :, :]
                 - wall_all.reshape(partitions, NV, TFP, BW_DEV).astype(jnp.float32)).astype(jnp.bfloat16)
    wall_jump = wall_jump.reshape(partitions, FW, BW_DEV)

    normal = jnp.concatenate([-jnp.ones((CF,), jnp.float32), jnp.ones((CF,), jnp.float32)])
    slot_index = jnp.arange(CF, dtype=jnp.int32)

    def finish(device):
        tet_block = lax.dynamic_slice_in_dim(tet_state, device * ET, ET, 1)
        tet_div = product(tet_volume, square_half(tet_block))
        codes = lax.dynamic_slice_in_dim(face_code, device * slots, slots, 0)
        counts = face_count[device]
        active = (slot_index[None, :] < counts[:, None]).reshape(slots)
        areas = lax.dynamic_slice_in_dim(face_area, device * slots, slots, 0)
        left_rows = left_all[device].astype(jnp.float32)
        right_rows = right_all[device].astype(jnp.float32)
        speed = jnp.maximum(jnp.abs(left_rows), jnp.abs(right_rows))
        flux_jump = 0.25 * normal * (right_rows * right_rows - left_rows * left_rows) - 0.5 * speed * (right_rows - left_rows)
        jump_rows = (jnp.where(active, areas, jnp.zeros_like(areas)) * flux_jump).astype(jnp.bfloat16)
        chosen = (codes % 4)[None, :] == face_ids[:, None]
        placed = jnp.where(chosen[:, None, :], jump_rows[None, :, :], jnp.zeros((4, FW, slots), jnp.bfloat16)).reshape(4 * FW, slots)
        tet_lift = product(face_lift, placed)
        tet_total = tet_div.at[:, codes // 4].add(tet_lift)
        tet_out = (tet_block.astype(jnp.float32) - section_step * tet_total).astype(jnp.bfloat16)
        prism_block = lax.dynamic_slice_in_dim(prism_state, device * EP, EP, 1)
        prism_div = product(prism_volume, square_half(prism_block))
        prism_index = lax.dynamic_slice_in_dim(burn_prism, device * BW_DEV, BW_DEV, 0)
        prism_lift = product(wall_lift, wall_jump[device])
        prism_total = prism_div.at[:, prism_index].add(prism_lift)
        prism_out = (prism_block.astype(jnp.float32) - section_step * prism_total).astype(jnp.bfloat16)
        return tet_out, prism_out

    tet_parts, prism_parts = lax.map(finish, jnp.arange(partitions, dtype=jnp.int32))
    tet_new = jnp.moveaxis(tet_parts, 0, 1).reshape(TW, TETS)
    prism_new = jnp.moveaxis(prism_parts, 0, 1).reshape(PW, PRISMS)
    return (tet_new, prism_new)
```

```python
import functools

import jax
import jax.numpy as jnp
from jax import lax
from jax.experimental import pallas as pl
from jax.experimental.pallas import tpu as pltpu
from jax.sharding import PartitionSpec as P

NV = 5
TFP = 15
FACES = 4
FACE_PAD = 80
VAR_PAD = 16
OWNER_ROWS = 8
CHUNK = 256

section_step = 0.25
F32 = jnp.float32
BF16 = jnp.bfloat16


def dot(left, right):
    return jnp.dot(left, right, preferred_element_type=F32)


def dot_t(left, right):
    return lax.dot_general(left, right, (((1,), (1,)), ((), ())), preferred_element_type=F32)


def square_half(values):
    widened = values.astype(F32)
    return (0.5 * widened * widened).astype(BF16)


def spread(groups, width, padded):
    row = lax.broadcasted_iota(jnp.int32, (groups * padded, groups * width), 0)
    column = lax.broadcasted_iota(jnp.int32, (groups * padded, groups * width), 1)
    group = jnp.zeros_like(row)
    for g in range(1, groups):
        group = group + (row >= g * padded).astype(jnp.int32)
    hit = (column == row - group * (padded - width)) & (row - group * padded < width)
    return jnp.where(hit, 1.0, 0.0).astype(BF16)


def one_hot(index, base, rows):
    row = lax.broadcasted_iota(jnp.int32, (rows, index.shape[1]), 0) + base
    return jnp.where(row == index, 1.0, 0.0).astype(BF16)


def kernel(
    n_axial,
    n_azim,
    tet_ref,
    prism_ref,
    tet_volume,
    prism_volume,
    face_extrap,
    face_lift,
    wall_extrap,
    wall_lift,
    code_ref,
    area_ref,
    burn_ref,
    owner_ref,
    count_ref,
    law_ref,
    tet_out,
    prism_out,
    hot,
    send,
    recv,
    div,
    part,
    parts,
    send_sem,
    recv_sem,
    part_send_sem,
    part_recv_sem,
):
    axial = lax.axis_index("axial")
    azim = lax.axis_index("azim")
    has_low = axial > 0
    has_high = axial < n_axial - 1
    low = (jnp.maximum(axial - 1, 0), azim)
    high = (jnp.minimum(axial + 1, n_axial - 1), azim)
    others = [(axial, lax.rem(azim + d, n_azim)) for d in range(1, n_azim)]
    mesh_id = pl.DeviceIdType.MESH

    barrier = pltpu.get_barrier_semaphore()

    @pl.when(has_low)
    def _():
        pl.semaphore_signal(barrier, inc=1, device_id=low, device_id_type=mesh_id)

    @pl.when(has_high)
    def _():
        pl.semaphore_signal(barrier, inc=1, device_id=high, device_id_type=mesh_id)

    for other in others:
        pl.semaphore_signal(barrier, inc=1, device_id=other, device_id_type=mesh_id)

    tets = tet_ref.shape[1]
    prisms = prism_ref.shape[1]
    slots = code_ref.shape[1]
    half = slots // 2

    code = code_ref[...]
    tet_index = code // FACES
    face = code - FACES * tet_index
    tet_state = tet_ref[...]
    faces_spread = spread(FACES, face_extrap.shape[0] // FACES, FACE_PAD)
    extrap = dot(faces_spread, face_extrap[...]).astype(BF16)
    lift = dot_t(face_lift[...], faces_spread).astype(BF16)
    for first in range(0, slots, CHUNK):
        lanes = slice(first, first + CHUNK)
        for base in range(0, tets, CHUNK):
            hot[base : base + CHUNK, lanes] = one_hot(tet_index[:, lanes], base, CHUNK)
        columns = dot(tet_state, hot[:, lanes]).astype(BF16)
        extended = dot(extrap, columns)
        rows = extended[0:FACE_PAD]
        for f in range(1, FACES):
            rows = jnp.where(
                face[:, lanes] == f, extended[f * FACE_PAD : (f + 1) * FACE_PAD], rows
            )
        side, offset = first // half, first % half
        send[side, :, offset : offset + CHUNK] = rows.astype(BF16)

    @pl.when(has_low & has_high)
    def _():
        pl.semaphore_wait(barrier, n_azim + 1)

    @pl.when(jnp.logical_not(has_low & has_high))
    def _():
        pl.semaphore_wait(barrier, n_azim)

    def face_copy(side, device):
        return pltpu.make_async_remote_copy(
            src_ref=send.at[side],
            dst_ref=recv.at[1 - side],
            send_sem=send_sem.at[side],
            recv_sem=recv_sem.at[1 - side],
            device_id=device,
            device_id_type=mesh_id,
        )

    @pl.when(has_low)
    def _():
        face_copy(0, low).start()

    @pl.when(has_high)
    def _():
        face_copy(1, high).start()

    wall_spread = spread(NV, TFP, VAR_PAD)
    wall_out = dot(wall_spread, wall_extrap[...]).astype(BF16)
    wall_in = dot_t(wall_lift[...], wall_spread).astype(BF16)
    prism_state = prism_ref[...]
    wall_rows = dot(wall_out, prism_state).astype(BF16).astype(F32)
    squares = wall_rows[(NV - 1) * VAR_PAD : NV * VAR_PAD]
    squares = squares * squares
    owner_row = lax.broadcasted_iota(jnp.int32, (OWNER_ROWS, owner_ref.shape[1]), 0)
    owner_hot = jnp.where(owner_row == owner_ref[...], 1.0, 0.0).astype(BF16)
    owned = dot_t(owner_hot, one_hot(burn_ref[...], 0, prisms))
    partial = jnp.sum(owned * jnp.sum(squares, axis=0, keepdims=True), axis=1, keepdims=True)
    part[...] = jnp.broadcast_to(partial, part.shape)

    def part_copy(source, d):
        return pltpu.make_async_remote_copy(
            src_ref=part,
            dst_ref=parts.at[source],
            send_sem=part_send_sem.at[d],
            recv_sem=part_recv_sem.at[source],
            device_id=others[d],
            device_id_type=mesh_id,
        )

    for d in range(n_azim - 1):
        part_copy(azim, d).start()

    div[...] = dot(prism_volume[...], square_half(prism_state))
    tet_flux = square_half(tet_state)

    @pl.when(has_low)
    def _():
        face_copy(0, low).wait_send()
        face_copy(1, low).wait_recv()

    @pl.when(jnp.logical_not(has_low))
    def _():
        recv[0] = jnp.zeros(recv.shape[1:], BF16)

    @pl.when(has_high)
    def _():
        face_copy(1, high).wait_send()
        face_copy(0, high).wait_recv()

    @pl.when(jnp.logical_not(has_high))
    def _():
        recv[1] = jnp.zeros(recv.shape[1:], BF16)

    slot = lax.broadcasted_iota(jnp.int32, (1, half), 1)
    jumps = []
    for side in range(2):
        lanes = slice(side * half, (side + 1) * half)
        left = send[side].astype(F32)
        right = recv[side].astype(F32)
        speed = jnp.maximum(jnp.abs(left), jnp.abs(right))
        step = right - left
        normal = 0.25 if side else -0.25
        flux_jump = normal * (right * right - left * left) - 0.5 * speed * step
        area = jnp.where(slot < count_ref[0, side], area_ref[:, lanes], 0.0)
        jumps.append((area * flux_jump).astype(BF16))
    jump = jnp.concatenate(jumps, axis=1)
    zero = jnp.zeros_like(jump)
    placed = jnp.concatenate([jnp.where(face == f, jump, zero) for f in range(FACES)], axis=0)
    for first in range(0, tets, CHUNK):
        lanes = slice(first, first + CHUNK)
        on_tets = dot_t(placed, hot[lanes, :]).astype(BF16)
        total = dot(tet_volume[...], tet_flux[:, lanes]) + dot(lift, on_tets)
        tet_out[:, lanes] = (tet_state[:, lanes].astype(F32) - section_step * total).astype(BF16)

    sums = part[...]
    for d in range(n_azim - 1):
        part_copy(azim, d).wait_send()
        source = others[d][1]
        part_copy(source, d).wait_recv()
        sums = sums + parts[source]
    faces = owner_ref.shape[1]
    inject = [jnp.zeros((1, prisms), F32) for _ in range(NV)]
    walls = jnp.zeros((1, prisms), F32)
    for o in range(n_azim):
        burn = law_ref[o, 0]
        damping = 1.0 / (1.0 + burn * sums[o : o + 1, 0:1] / (faces * TFP))
        scale = owned[o : o + 1] * (burn * damping)
        walls = walls + owned[o : o + 1]
        for v in range(NV):
            inject[v] = inject[v] + law_ref[o, 1 + v] * scale
    wall_jump = jnp.concatenate(
        [
            jnp.where(
                walls > 0.5,
                inject[v] * squares - wall_rows[v * VAR_PAD : (v + 1) * VAR_PAD],
                0.0,
            )
            for v in range(NV)
        ],
        axis=0,
    ).astype(BF16)
    for first in range(0, prisms, CHUNK):
        lanes = slice(first, first + CHUNK)
        total = div[:, lanes] + dot(wall_in, wall_jump[:, lanes])
        prism_out[:, lanes] = (
            prism_state[:, lanes].astype(F32) - section_step * total
        ).astype(BF16)


def on_device(
    n_axial,
    n_azim,
    tet_state,
    prism_state,
    tet_volume,
    prism_volume,
    face_extrap,
    face_lift,
    wall_extrap,
    wall_lift,
    face_code,
    face_count,
    face_area,
    burn_prism,
    burn_owner,
    burn_law,
):
    slots = face_code.shape[0]
    faces = burn_prism.shape[0]
    vmem = pl.BlockSpec(memory_space=pltpu.VMEM)
    smem = pl.BlockSpec(memory_space=pltpu.SMEM)
    return pl.pallas_call(
        functools.partial(kernel, n_axial, n_azim),
        out_shape=(
            jax.ShapeDtypeStruct(tet_state.shape, BF16),
            jax.ShapeDtypeStruct(prism_state.shape, BF16),
        ),
        in_specs=[vmem] * 12 + [smem] * 2,
        out_specs=(vmem, vmem),
        scratch_shapes=[
            pltpu.VMEM((tet_state.shape[1], slots), BF16),
            pltpu.VMEM((2, FACE_PAD, slots // 2), BF16),
            pltpu.VMEM((2, FACE_PAD, slots // 2), BF16),
            pltpu.VMEM(prism_state.shape, F32),
            pltpu.VMEM((OWNER_ROWS, 128), F32),
            pltpu.VMEM((n_azim, OWNER_ROWS, 128), F32),
            pltpu.SemaphoreType.DMA((2,)),
            pltpu.SemaphoreType.DMA((2,)),
            pltpu.SemaphoreType.DMA((n_azim - 1,)),
            pltpu.SemaphoreType.DMA((n_azim,)),
        ],
        compiler_params=pltpu.CompilerParams(
            collective_id=0, has_side_effects=True, vmem_limit_bytes=48 * 1024 * 1024
        ),
    )(
        tet_state,
        prism_state,
        tet_volume,
        prism_volume,
        face_extrap,
        face_lift,
        wall_extrap,
        wall_lift,
        face_code.reshape(1, slots),
        face_area.reshape(1, slots),
        burn_prism.reshape(1, faces),
        burn_owner.reshape(1, faces),
        face_count,
        burn_law[0],
    )


def solution(mesh):
    placed = (
        P(None, ("axial", "azim")),
        P(None, ("axial", "azim")),
        P(),
        P(),
        P(),
        P(),
        P(),
        P(),
        P(("axial", "azim")),
        P(("axial", "azim"), None),
        P(("axial", "azim")),
        P(("axial", "azim")),
        P(("axial", "azim"), None),
        P("axial", None, None),
    )
    return jax.shard_map(
        functools.partial(on_device, mesh.shape["axial"], mesh.shape["azim"]),
        mesh=mesh,
        in_specs=placed,
        out_specs=(P(None, ("axial", "azim")), P(None, ("axial", "azim"))),
        check_vma=False,
    )
```

```python
import functools

import jax
import jax.numpy as jnp
from jax import lax
from jax.experimental import pallas as pl
from jax.experimental.pallas import tpu as pltpu
from jax.sharding import PartitionSpec as P

NV = 5
TFP = 15
FACES = 4
FACE_PAD = 80
VAR_PAD = 16
OWNER_ROWS = 8
CHUNK = 256
VMEM_LIMIT = 63 * 1024 * 1024

section_step = 0.25
F32 = jnp.float32
BF16 = jnp.bfloat16


def dot(left, right):
    return jnp.dot(left, right, preferred_element_type=F32)


def dot_t(left, right):
    return lax.dot_general(left, right, (((1,), (1,)), ((), ())), preferred_element_type=F32)


def square_half(values):
    widened = values.astype(F32)
    return (0.5 * widened * widened).astype(BF16)


def spread(groups, width, padded):
    row = lax.broadcasted_iota(jnp.int32, (groups * padded, groups * width), 0)
    column = lax.broadcasted_iota(jnp.int32, (groups * padded, groups * width), 1)
    group = jnp.zeros_like(row)
    for g in range(1, groups):
        group = group + (row >= g * padded).astype(jnp.int32)
    hit = (column == row - group * (padded - width)) & (row - group * padded < width)
    return jnp.where(hit, 1.0, 0.0).astype(BF16)


def one_hot(index, base, rows):
    row = lax.broadcasted_iota(jnp.int32, (rows, index.shape[1]), 0) + base
    return jnp.where(row == index, 1.0, 0.0).astype(BF16)


def kernel(
    n_axial,
    n_azim,
    tet_hbm,
    prism_hbm,
    tet_volume_hbm,
    prism_volume_hbm,
    face_extrap_hbm,
    face_lift_hbm,
    wall_extrap_hbm,
    wall_lift_hbm,
    code_hbm,
    area_hbm,
    burn_hbm,
    owner_hbm,
    count_hbm,
    law_hbm,
    tet_out_hbm,
    prism_out_hbm,
    hot,
    tet_base,
    prism_base,
    tet_out,
    prism_out,
    tet_ref,
    prism_ref,
    tet_volume,
    prism_volume,
    face_extrap,
    face_lift,
    wall_extrap,
    wall_lift,
    code_ref,
    area_ref,
    burn_ref,
    owner_ref,
    count_ref,
    law_ref,
    send,
    recv,
    part,
    parts,
    load_sem,
    store_sem,
    send_sem,
    recv_sem,
    part_send_sem,
    part_recv_sem,
):
    axial = lax.axis_index("axial")
    azim = lax.axis_index("azim")
    has_low = axial > 0
    has_high = axial < n_axial - 1
    low = (jnp.maximum(axial - 1, 0), azim)
    high = (jnp.minimum(axial + 1, n_axial - 1), azim)
    others = [(axial, lax.rem(azim + d, n_azim)) for d in range(1, n_azim)]
    mesh_id = pl.DeviceIdType.MESH

    loads = [
        pltpu.make_async_copy(source, target, load_sem.at[i])
        for i, (source, target) in enumerate(
            (
                (code_hbm, code_ref),
                (tet_hbm, tet_ref),
                (face_extrap_hbm, face_extrap),
                (prism_hbm, prism_ref),
                (wall_extrap_hbm, wall_extrap),
                (burn_hbm, burn_ref),
                (owner_hbm, owner_ref),
                (prism_volume_hbm, prism_volume),
                (tet_volume_hbm, tet_volume),
                (face_lift_hbm, face_lift),
                (wall_lift_hbm, wall_lift),
                (area_hbm, area_ref),
                (count_hbm, count_ref),
                (law_hbm, law_ref),
            )
        )
    ]
    for load in loads:
        load.start()

    barrier = pltpu.get_barrier_semaphore()

    @pl.when(has_low)
    def _():
        pl.semaphore_signal(barrier, inc=1, device_id=low, device_id_type=mesh_id)

    @pl.when(has_high)
    def _():
        pl.semaphore_signal(barrier, inc=1, device_id=high, device_id_type=mesh_id)

    for other in others:
        pl.semaphore_signal(barrier, inc=1, device_id=other, device_id_type=mesh_id)

    tets = tet_ref.shape[1]
    prisms = prism_ref.shape[1]
    slots = code_ref.shape[1]
    half = slots // 2
    faces_spread = spread(FACES, face_extrap.shape[1] // FACES, FACE_PAD)
    wall_spread = spread(NV, TFP, VAR_PAD)

    def face_copy(side, device):
        return pltpu.make_async_remote_copy(
            src_ref=send.at[side],
            dst_ref=recv.at[1 - side],
            send_sem=send_sem.at[side],
            recv_sem=recv_sem.at[1 - side],
            device_id=device,
            device_id_type=mesh_id,
        )

    for load in loads[0:3]:
        load.wait()
    code = code_ref[...]
    tet_index = code // FACES
    face = code - FACES * tet_index
    tet_state = tet_ref[...]
    extrap = dot_t(faces_spread, face_extrap[...]).astype(BF16)
    for first in range(0, slots, CHUNK):
        lanes = slice(first, first + CHUNK)
        for base in range(0, tets, CHUNK):
            hot[base : base + CHUNK, lanes] = one_hot(tet_index[:, lanes], base, CHUNK)
        columns = dot(tet_state, hot[:, lanes]).astype(BF16)
        extended = dot(extrap, columns)
        rows = extended[0:FACE_PAD]
        for f in range(1, FACES):
            rows = jnp.where(
                face[:, lanes] == f, extended[f * FACE_PAD : (f + 1) * FACE_PAD], rows
            )
        side, offset = first // half, first % half
        send[side, :, offset : offset + CHUNK] = rows.astype(BF16)
        if offset + CHUNK < half:
            continue
        if side == 0:

            @pl.when(has_low & has_high)
            def _():
                pl.semaphore_wait(barrier, n_azim + 1)

            @pl.when(jnp.logical_not(has_low & has_high))
            def _():
                pl.semaphore_wait(barrier, n_azim)

            @pl.when(has_low)
            def _():
                face_copy(0, low).start()

        else:

            @pl.when(has_high)
            def _():
                face_copy(1, high).start()

    for load in loads[3:7]:
        load.wait()
    wall_out = dot(wall_spread, wall_extrap[...]).astype(BF16)
    prism_state = prism_ref[...]
    wall_rows = dot(wall_out, prism_state).astype(BF16).astype(F32)
    squares = wall_rows[(NV - 1) * VAR_PAD : NV * VAR_PAD]
    squares = squares * squares
    owner_row = lax.broadcasted_iota(jnp.int32, (OWNER_ROWS, owner_ref.shape[1]), 0)
    owner_hot = jnp.where(owner_row == owner_ref[...], 1.0, 0.0).astype(BF16)
    owned = dot_t(owner_hot, one_hot(burn_ref[...], 0, prisms))
    partial = jnp.sum(owned * jnp.sum(squares, axis=0, keepdims=True), axis=1, keepdims=True)
    part[...] = jnp.broadcast_to(partial, part.shape)

    def part_copy(source, d):
        return pltpu.make_async_remote_copy(
            src_ref=part,
            dst_ref=parts.at[source],
            send_sem=part_send_sem.at[d],
            recv_sem=part_recv_sem.at[source],
            device_id=others[d],
            device_id_type=mesh_id,
        )

    for d in range(n_azim - 1):
        part_copy(azim, d).start()

    for load in loads[7:]:
        load.wait()
    prism_base[...] = prism_state.astype(F32) - section_step * dot(
        prism_volume[...], square_half(prism_state)
    )
    tet_base[...] = tet_state.astype(F32) - section_step * dot(
        tet_volume[...], square_half(tet_state)
    )
    lift = dot_t(face_lift[...], faces_spread).astype(BF16)
    wall_in = lax.dot_general(
        wall_lift[...], wall_spread, (((0,), (1,)), ((), ())), preferred_element_type=F32
    ).astype(BF16)

    sums = part[...]
    for d in range(n_azim - 1):
        part_copy(azim, d).wait_send()
        source = others[d][1]
        part_copy(source, d).wait_recv()
        sums = sums + parts[source]
    faces = owner_ref.shape[1]
    inject = [jnp.zeros((1, prisms), F32) for _ in range(NV)]
    walls = jnp.zeros((1, prisms), F32)
    for o in range(n_azim):
        burn = law_ref[o : o + 1, 0:1]
        damping = 1.0 / (1.0 + burn * sums[o : o + 1, 0:1] / (faces * TFP))
        scale = owned[o : o + 1] * (burn * damping)
        walls = walls + owned[o : o + 1]
        for v in range(NV):
            inject[v] = inject[v] + law_ref[o : o + 1, 1 + v : 2 + v] * scale
    wall_jump = jnp.concatenate(
        [
            jnp.where(
                walls > 0.5,
                inject[v] * squares - wall_rows[v * VAR_PAD : (v + 1) * VAR_PAD],
                0.0,
            ).astype(BF16)
            for v in range(NV)
        ],
        axis=0,
    )
    stores = []

    def store(out, hbm, first):
        lanes = pl.ds(first, CHUNK)
        copy = pltpu.make_async_copy(
            out.at[:, lanes], hbm.at[:, lanes], store_sem.at[len(stores)]
        )
        copy.start()
        stores.append(copy)

    for first in range(0, prisms, CHUNK):
        lanes = slice(first, first + CHUNK)
        lifted = dot(wall_in, wall_jump[:, lanes])
        prism_out[:, lanes] = (prism_base[:, lanes] - section_step * lifted).astype(BF16)
        store(prism_out, prism_out_hbm, first)

    @pl.when(has_low)
    def _():
        face_copy(0, low).wait_send()
        face_copy(1, low).wait_recv()

    @pl.when(jnp.logical_not(has_low))
    def _():
        recv[0] = jnp.zeros(recv.shape[1:], BF16)

    @pl.when(has_high)
    def _():
        face_copy(1, high).wait_send()
        face_copy(0, high).wait_recv()

    @pl.when(jnp.logical_not(has_high))
    def _():
        recv[1] = jnp.zeros(recv.shape[1:], BF16)

    slot = lax.broadcasted_iota(jnp.int32, (1, half), 1)
    jumps = []
    for side in range(2):
        lanes = slice(side * half, (side + 1) * half)
        left = send[side].astype(F32)
        right = recv[side].astype(F32)
        speed = jnp.maximum(jnp.abs(left), jnp.abs(right))
        step = right - left
        normal = 0.25 if side else -0.25
        flux_jump = normal * (right * right - left * left) - 0.5 * speed * step
        live = slot < count_ref[0:1, side : side + 1]
        area = jnp.where(live, area_ref[:, lanes], 0.0)
        jumps.append((area * flux_jump).astype(BF16))
    jump = jnp.concatenate(jumps, axis=1)
    zero = jnp.zeros_like(jump)
    placed = jnp.concatenate([jnp.where(face == f, jump, zero) for f in range(FACES)], axis=0)
    for first in range(0, tets, CHUNK):
        lanes = slice(first, first + CHUNK)
        on_tets = dot_t(placed, hot[lanes, :]).astype(BF16)
        lifted = dot(lift, on_tets)
        tet_out[:, lanes] = (tet_base[:, lanes] - section_step * lifted).astype(BF16)
        store(tet_out, tet_out_hbm, first)
    for copy in stores:
        copy.wait()


def on_device(
    n_axial,
    n_azim,
    tet_state,
    prism_state,
    tet_volume,
    prism_volume,
    face_extrap,
    face_lift,
    wall_extrap,
    wall_lift,
    face_code,
    face_count,
    face_area,
    burn_prism,
    burn_owner,
    burn_law,
):
    slots = face_code.shape[0]
    faces = burn_prism.shape[0]
    tets = tet_state.shape[1]
    prisms = prism_state.shape[1]
    hbm = pl.BlockSpec(memory_space=pltpu.HBM)
    operands = (
        tet_state,
        prism_state,
        tet_volume,
        prism_volume,
        face_extrap.T,
        face_lift,
        wall_extrap,
        wall_lift.T,
        face_code.reshape(1, slots),
        face_area.reshape(1, slots),
        burn_prism.reshape(1, faces),
        burn_owner.reshape(1, faces),
        face_count,
        burn_law[0],
    )
    return pl.pallas_call(
        functools.partial(kernel, n_axial, n_azim),
        out_shape=(
            jax.ShapeDtypeStruct(tet_state.shape, BF16),
            jax.ShapeDtypeStruct(prism_state.shape, BF16),
        ),
        in_specs=[hbm] * len(operands),
        out_specs=(hbm, hbm),
        scratch_shapes=[
            pltpu.VMEM((tets, slots), BF16),
            pltpu.VMEM(tet_state.shape, F32),
            pltpu.VMEM(prism_state.shape, F32),
            pltpu.VMEM(tet_state.shape, BF16),
            pltpu.VMEM(prism_state.shape, BF16),
        ]
        + [pltpu.VMEM(x.shape, x.dtype) for x in operands]
        + [
            pltpu.VMEM((2, FACE_PAD, slots // 2), BF16),
            pltpu.VMEM((2, FACE_PAD, slots // 2), BF16),
            pltpu.VMEM((OWNER_ROWS, 128), F32),
            pltpu.VMEM((n_azim, OWNER_ROWS, 128), F32),
            pltpu.SemaphoreType.DMA((len(operands),)),
            pltpu.SemaphoreType.DMA((tets // CHUNK + prisms // CHUNK,)),
            pltpu.SemaphoreType.DMA((2,)),
            pltpu.SemaphoreType.DMA((2,)),
            pltpu.SemaphoreType.DMA((n_azim - 1,)),
            pltpu.SemaphoreType.DMA((n_azim,)),
        ],
        compiler_params=pltpu.CompilerParams(
            collective_id=0, has_side_effects=True, vmem_limit_bytes=VMEM_LIMIT
        ),
    )(*operands)


def solution(mesh):
    placed = (
        P(None, ("axial", "azim")),
        P(None, ("axial", "azim")),
        P(),
        P(),
        P(),
        P(),
        P(),
        P(),
        P(("axial", "azim")),
        P(("axial", "azim"), None),
        P(("axial", "azim")),
        P(("axial", "azim")),
        P(("axial", "azim"), None),
        P("axial", None, None),
    )
    return jax.shard_map(
        functools.partial(on_device, mesh.shape["axial"], mesh.shape["azim"]),
        mesh=mesh,
        in_specs=placed,
        out_specs=(P(None, ("axial", "azim")), P(None, ("axial", "azim"))),
        check_vma=False,
    )
```

```python
import functools

import jax
import jax.numpy as jnp
from jax import lax
from jax.experimental import pallas as pl
from jax.experimental.pallas import tpu as pltpu
from jax.sharding import PartitionSpec as P

NV = 5
TFP = 15
FACES = 4
FACE_PAD = 80
VAR_PAD = 16
OWNER_ROWS = 8
CHUNK = 256
VMEM_LIMIT = 63 * 1024 * 1024
HAND_ROWS = 96
HAND_LIMIT = 63 * 1024 * 1024

section_step = 0.25
F32 = jnp.float32
BF16 = jnp.bfloat16


def dot(left, right):
    return jnp.dot(left, right, preferred_element_type=F32)


def dot_t(left, right):
    return lax.dot_general(left, right, (((1,), (1,)), ((), ())), preferred_element_type=F32)


def square_half(values):
    widened = values.astype(F32)
    return (0.5 * widened * widened).astype(BF16)


def spread(groups, width, padded):
    row = lax.broadcasted_iota(jnp.int32, (groups * padded, groups * width), 0)
    column = lax.broadcasted_iota(jnp.int32, (groups * padded, groups * width), 1)
    group = jnp.zeros_like(row)
    for g in range(1, groups):
        group = group + (row >= g * padded).astype(jnp.int32)
    hit = (column == row - group * (padded - width)) & (row - group * padded < width)
    return jnp.where(hit, 1.0, 0.0).astype(BF16)


def one_hot(index, base, rows):
    row = lax.broadcasted_iota(jnp.int32, (rows, index.shape[1]), 0) + base
    return jnp.where(row == index, 1.0, 0.0).astype(BF16)


def kernel(
    n_axial,
    n_azim,
    tet_hbm,
    prism_hbm,
    tet_volume_hbm,
    prism_volume_hbm,
    face_extrap_hbm,
    face_lift_hbm,
    wall_extrap_hbm,
    wall_lift_hbm,
    code_hbm,
    area_hbm,
    burn_hbm,
    owner_hbm,
    count_hbm,
    law_hbm,
    tet_out_hbm,
    prism_out_hbm,
    hot,
    tet_base,
    prism_base,
    tet_out,
    prism_out,
    tet_ref,
    prism_ref,
    tet_volume,
    prism_volume,
    face_extrap,
    face_lift,
    wall_extrap,
    wall_lift,
    code_ref,
    area_ref,
    burn_ref,
    owner_ref,
    count_ref,
    law_ref,
    send,
    recv,
    part,
    parts,
    load_sem,
    store_sem,
    send_sem,
    recv_sem,
    part_send_sem,
    part_recv_sem,
):
    axial = lax.axis_index("axial")
    azim = lax.axis_index("azim")
    has_low = axial > 0
    has_high = axial < n_axial - 1
    low = (jnp.maximum(axial - 1, 0), azim)
    high = (jnp.minimum(axial + 1, n_axial - 1), azim)
    others = [(axial, lax.rem(azim + d, n_azim)) for d in range(1, n_azim)]
    mesh_id = pl.DeviceIdType.MESH

    loads = [
        pltpu.make_async_copy(source, target, load_sem.at[i])
        for i, (source, target) in enumerate(
            (
                (face_extrap_hbm, face_extrap),
                (code_hbm, code_ref),
                (tet_hbm, tet_ref),
                (prism_hbm, prism_ref),
                (wall_extrap_hbm, wall_extrap),
                (burn_hbm, burn_ref),
                (owner_hbm, owner_ref),
                (prism_volume_hbm, prism_volume),
                (tet_volume_hbm, tet_volume),
                (face_lift_hbm, face_lift),
                (wall_lift_hbm, wall_lift),
                (area_hbm, area_ref),
                (count_hbm, count_ref),
                (law_hbm, law_ref),
            )
        )
    ]
    for load in loads:
        load.start()

    barrier = pltpu.get_barrier_semaphore()

    @pl.when(has_low)
    def _():
        pl.semaphore_signal(barrier, inc=1, device_id=low, device_id_type=mesh_id)

    @pl.when(has_high)
    def _():
        pl.semaphore_signal(barrier, inc=1, device_id=high, device_id_type=mesh_id)

    for other in others:
        pl.semaphore_signal(barrier, inc=1, device_id=other, device_id_type=mesh_id)

    tets = tet_ref.shape[1]
    prisms = prism_ref.shape[1]
    slots = code_ref.shape[1]
    half = slots // 2
    faces_spread = spread(FACES, face_extrap.shape[1] // FACES, FACE_PAD)
    wall_spread = spread(NV, TFP, VAR_PAD)

    pieces = half // CHUNK

    def face_copy(side, piece, device):
        return pltpu.make_async_remote_copy(
            src_ref=send.at[side, piece],
            dst_ref=recv.at[1 - side, piece],
            send_sem=send_sem.at[side, piece],
            recv_sem=recv_sem.at[1 - side, piece],
            device_id=device,
            device_id_type=mesh_id,
        )

    loads[0].wait()
    extrap = dot_t(faces_spread, face_extrap[...]).astype(BF16)
    loads[1].wait()
    code = code_ref[...]
    tet_index = code // FACES
    face = code - FACES * tet_index
    greeted = False
    for piece in range(pieces):
        for side in range(2):
            first = side * half + piece * CHUNK
            lanes = slice(first, first + CHUNK)
            for base in range(0, tets, CHUNK):
                hot[base : base + CHUNK, lanes] = one_hot(tet_index[:, lanes], base, CHUNK)
            if not greeted:
                loads[2].wait()
            columns = dot(tet_ref[...], hot[:, lanes]).astype(BF16)
            extended = dot(extrap, columns)
            rows = extended[0:FACE_PAD]
            for f in range(1, FACES):
                rows = jnp.where(
                    face[:, lanes] == f, extended[f * FACE_PAD : (f + 1) * FACE_PAD], rows
                )
            send[side, piece] = rows.astype(BF16)
            if not greeted:
                greeted = True

                @pl.when(has_low & has_high)
                def _():
                    pl.semaphore_wait(barrier, n_azim + 1)

                @pl.when(jnp.logical_not(has_low & has_high))
                def _():
                    pl.semaphore_wait(barrier, n_azim)

            @pl.when(has_high if side else has_low)
            def _():
                face_copy(side, piece, high if side else low).start()

    for load in loads[3:7]:
        load.wait()
    wall_out = dot(wall_spread, wall_extrap[...]).astype(BF16)
    prism_state = prism_ref[...]
    wall_rows = dot(wall_out, prism_state).astype(BF16).astype(F32)
    squares = wall_rows[(NV - 1) * VAR_PAD : NV * VAR_PAD]
    squares = squares * squares
    owner_row = lax.broadcasted_iota(jnp.int32, (OWNER_ROWS, owner_ref.shape[1]), 0)
    owner_hot = jnp.where(owner_row == owner_ref[...], 1.0, 0.0).astype(BF16)
    owned = dot_t(owner_hot, one_hot(burn_ref[...], 0, prisms))
    partial = jnp.sum(owned * jnp.sum(squares, axis=0, keepdims=True), axis=1, keepdims=True)
    part[...] = jnp.broadcast_to(partial, part.shape)

    def part_copy(source, d):
        return pltpu.make_async_remote_copy(
            src_ref=part,
            dst_ref=parts.at[source],
            send_sem=part_send_sem.at[d],
            recv_sem=part_recv_sem.at[source],
            device_id=others[d],
            device_id_type=mesh_id,
        )

    for d in range(n_azim - 1):
        part_copy(azim, d).start()

    for load in loads[7:]:
        load.wait()
    prism_base[...] = prism_state.astype(F32) - section_step * dot(
        prism_volume[...], square_half(prism_state)
    )
    tet_state = tet_ref[...]
    tet_base[...] = tet_state.astype(F32) - section_step * dot(
        tet_volume[...], square_half(tet_state)
    )
    lift = dot_t(face_lift[...], faces_spread).astype(BF16)
    wall_in = lax.dot_general(
        wall_lift[...], wall_spread, (((0,), (1,)), ((), ())), preferred_element_type=F32
    ).astype(BF16)

    sums = part[...]
    for d in range(n_azim - 1):
        part_copy(azim, d).wait_send()
        source = others[d][1]
        part_copy(source, d).wait_recv()
        sums = sums + parts[source]
    faces = owner_ref.shape[1]
    inject = [jnp.zeros((1, prisms), F32) for _ in range(NV)]
    walls = jnp.zeros((1, prisms), F32)
    for o in range(n_azim):
        burn = law_ref[o : o + 1, 0:1]
        damping = 1.0 / (1.0 + burn * sums[o : o + 1, 0:1] / (faces * TFP))
        scale = owned[o : o + 1] * (burn * damping)
        walls = walls + owned[o : o + 1]
        for v in range(NV):
            inject[v] = inject[v] + law_ref[o : o + 1, 1 + v : 2 + v] * scale
    wall_jump = jnp.concatenate(
        [
            jnp.where(
                walls > 0.5,
                inject[v] * squares - wall_rows[v * VAR_PAD : (v + 1) * VAR_PAD],
                0.0,
            ).astype(BF16)
            for v in range(NV)
        ],
        axis=0,
    )
    stores = []

    def store(out, hbm, first):
        lanes = pl.ds(first, CHUNK)
        copy = pltpu.make_async_copy(
            out.at[:, lanes], hbm.at[:, lanes], store_sem.at[len(stores)]
        )
        copy.start()
        stores.append(copy)

    for first in range(0, prisms, CHUNK):
        lanes = slice(first, first + CHUNK)
        lifted = dot(wall_in, wall_jump[:, lanes])
        prism_out[:, lanes] = (prism_base[:, lanes] - section_step * lifted).astype(BF16)
        store(prism_out, prism_out_hbm, first)

    slot = lax.broadcasted_iota(jnp.int32, (1, CHUNK), 1)
    for piece in range(pieces):
        for side in range(2):
            first = side * half + piece * CHUNK
            lanes = slice(first, first + CHUNK)
            has, device = (has_high, high) if side else (has_low, low)

            @pl.when(has)
            def _():
                face_copy(side, piece, device).wait_send()
                face_copy(1 - side, piece, device).wait_recv()

            @pl.when(jnp.logical_not(has))
            def _():
                recv[side, piece] = jnp.zeros(recv.shape[2:], BF16)

            left = send[side, piece].astype(F32)
            right = recv[side, piece].astype(F32)
            speed = jnp.maximum(jnp.abs(left), jnp.abs(right))
            step = right - left
            normal = 0.25 if side else -0.25
            flux_jump = normal * (right * right - left * left) - 0.5 * speed * step
            live = slot + piece * CHUNK < count_ref[0:1, side : side + 1]
            area = jnp.where(live, area_ref[:, lanes], 0.0)
            jump = (area * flux_jump).astype(BF16)
            zero = jnp.zeros_like(jump)
            placed = jnp.concatenate(
                [jnp.where(face[:, lanes] == f, jump, zero) for f in range(FACES)], axis=0
            )
            last = side == 1 and piece == pieces - 1
            for base in range(0, tets, CHUNK):
                there = slice(base, base + CHUNK)
                on_tets = dot_t(placed, hot[there, lanes]).astype(BF16)
                total = tet_base[:, there] - section_step * dot(lift, on_tets)
                if last:
                    tet_out[:, there] = total.astype(BF16)
                    store(tet_out, tet_out_hbm, base)
                else:
                    tet_base[:, there] = total
    for copy in stores:
        copy.wait()


def hand_over(tet_new, prism_new, tet_out, prism_out, sem):
    copies = []
    for source, target in ((prism_new, prism_out), (tet_new, tet_out)):
        for first in range(0, source.shape[0], HAND_ROWS):
            rows = pl.ds(first, min(HAND_ROWS, source.shape[0] - first))
            copy = pltpu.make_async_copy(source.at[rows], target.at[rows], sem.at[len(copies)])
            copy.start()
            copies.append(copy)
    for copy in copies:
        copy.wait()


def on_device(
    n_axial,
    n_azim,
    tet_state,
    prism_state,
    tet_volume,
    prism_volume,
    face_extrap,
    face_lift,
    wall_extrap,
    wall_lift,
    face_code,
    face_count,
    face_area,
    burn_prism,
    burn_owner,
    burn_law,
):
    slots = face_code.shape[0]
    faces = burn_prism.shape[0]
    tets = tet_state.shape[1]
    prisms = prism_state.shape[1]
    hbm = pl.BlockSpec(memory_space=pltpu.HBM)
    operands = (
        tet_state,
        prism_state,
        tet_volume,
        prism_volume,
        face_extrap.T,
        face_lift,
        wall_extrap,
        wall_lift.T,
        face_code.reshape(1, slots),
        face_area.reshape(1, slots),
        burn_prism.reshape(1, faces),
        burn_owner.reshape(1, faces),
        face_count,
        burn_law[0],
    )
    results = pl.pallas_call(
        functools.partial(kernel, n_axial, n_azim),
        out_shape=(
            jax.ShapeDtypeStruct(tet_state.shape, BF16),
            jax.ShapeDtypeStruct(prism_state.shape, BF16),
        ),
        in_specs=[hbm] * len(operands),
        out_specs=(hbm, hbm),
        scratch_shapes=[
            pltpu.VMEM((tets, slots), BF16),
            pltpu.VMEM(tet_state.shape, F32),
            pltpu.VMEM(prism_state.shape, F32),
            pltpu.VMEM(tet_state.shape, BF16),
            pltpu.VMEM(prism_state.shape, BF16),
        ]
        + [pltpu.VMEM(x.shape, x.dtype) for x in operands]
        + [
            pltpu.VMEM((2, slots // 2 // CHUNK, FACE_PAD, CHUNK), BF16),
            pltpu.VMEM((2, slots // 2 // CHUNK, FACE_PAD, CHUNK), BF16),
            pltpu.VMEM((OWNER_ROWS, 128), F32),
            pltpu.VMEM((n_azim, OWNER_ROWS, 128), F32),
            pltpu.SemaphoreType.DMA((len(operands),)),
            pltpu.SemaphoreType.DMA((tets // CHUNK + prisms // CHUNK,)),
            pltpu.SemaphoreType.DMA((2, slots // 2 // CHUNK)),
            pltpu.SemaphoreType.DMA((2, slots // 2 // CHUNK)),
            pltpu.SemaphoreType.DMA((n_azim - 1,)),
            pltpu.SemaphoreType.DMA((n_azim,)),
        ],
        compiler_params=pltpu.CompilerParams(
            collective_id=0, has_side_effects=True, vmem_limit_bytes=VMEM_LIMIT
        ),
    )(*operands)
    return pl.pallas_call(
        hand_over,
        out_shape=tuple(jax.ShapeDtypeStruct(x.shape, x.dtype) for x in results),
        in_specs=(hbm, hbm),
        out_specs=(hbm, hbm),
        scratch_shapes=[pltpu.SemaphoreType.DMA((sum(-(-x.shape[0] // HAND_ROWS) for x in results),))],
        compiler_params=pltpu.CompilerParams(vmem_limit_bytes=HAND_LIMIT),
    )(*results)


def solution(mesh):
    placed = (
        P(None, ("axial", "azim")),
        P(None, ("axial", "azim")),
        P(),
        P(),
        P(),
        P(),
        P(),
        P(),
        P(("axial", "azim")),
        P(("axial", "azim"), None),
        P(("axial", "azim")),
        P(("axial", "azim")),
        P(("axial", "azim"), None),
        P("axial", None, None),
    )
    return jax.shard_map(
        functools.partial(on_device, mesh.shape["axial"], mesh.shape["azim"]),
        mesh=mesh,
        in_specs=placed,
        out_specs=(P(None, ("axial", "azim")), P(None, ("axial", "azim"))),
        check_vma=False,
    )
```

```python
import functools

import jax
import jax.numpy as jnp
from jax import lax
from jax.experimental import pallas as pl
from jax.experimental.pallas import tpu as pltpu
from jax.sharding import PartitionSpec as P

NV = 5
TFP = 15
FACES = 4
FACE_PAD = 80
VAR_PAD = 16
OWNER_ROWS = 8
CHUNK = 256
VMEM_LIMIT = 63 * 1024 * 1024

section_step = 0.25
F32 = jnp.float32
BF16 = jnp.bfloat16


def dot(left, right):
    return jnp.dot(left, right, preferred_element_type=F32)


def dot_t(left, right):
    return lax.dot_general(left, right, (((1,), (1,)), ((), ())), preferred_element_type=F32)


def square_half(values):
    widened = values.astype(F32)
    return (0.5 * widened * widened).astype(BF16)


def spread(groups, width, padded):
    row = lax.broadcasted_iota(jnp.int32, (groups * padded, groups * width), 0)
    column = lax.broadcasted_iota(jnp.int32, (groups * padded, groups * width), 1)
    group = jnp.zeros_like(row)
    for g in range(1, groups):
        group = group + (row >= g * padded).astype(jnp.int32)
    hit = (column == row - group * (padded - width)) & (row - group * padded < width)
    return jnp.where(hit, 1.0, 0.0).astype(BF16)


def one_hot(index, base, rows):
    row = lax.broadcasted_iota(jnp.int32, (rows, index.shape[1]), 0) + base
    return jnp.where(row == index, 1.0, 0.0).astype(BF16)


def load_all(pairs, sem):
    loads = [
        pltpu.make_async_copy(source, target, sem.at[i])
        for i, (source, target) in enumerate(pairs)
    ]
    for load in loads:
        load.start()
    return loads


def exchange(
    n_axial,
    n_azim,
    tet_hbm,
    prism_hbm,
    tet_volume_hbm,
    prism_volume_hbm,
    face_extrap_hbm,
    face_lift_hbm,
    wall_extrap_hbm,
    wall_lift_hbm,
    code_hbm,
    burn_hbm,
    owner_hbm,
    law_hbm,
    left_hbm,
    right_hbm,
    base_hbm,
    lift_hbm,
    prism_new_hbm,
    tet_ref,
    prism_ref,
    tet_volume,
    prism_volume,
    face_extrap,
    face_lift,
    wall_extrap,
    wall_lift,
    code_ref,
    burn_ref,
    owner_ref,
    law_ref,
    send,
    tet_base,
    lift,
    prism_new,
    hot,
    prism_base,
    part,
    parts,
    load_sem,
    store_sem,
    send_sem,
    recv_sem,
    part_send_sem,
    part_recv_sem,
):
    axial = lax.axis_index("axial")
    azim = lax.axis_index("azim")
    has_low = axial > 0
    has_high = axial < n_axial - 1
    low = (jnp.maximum(axial - 1, 0), azim)
    high = (jnp.minimum(axial + 1, n_axial - 1), azim)
    others = [(axial, lax.rem(azim + d, n_azim)) for d in range(1, n_azim)]
    mesh_id = pl.DeviceIdType.MESH

    loads = load_all(
        (
            (face_extrap_hbm, face_extrap),
            (code_hbm, code_ref),
            (tet_hbm, tet_ref),
            (burn_hbm, burn_ref),
            (owner_hbm, owner_ref),
            (wall_extrap_hbm, wall_extrap),
            (prism_hbm, prism_ref),
            (prism_volume_hbm, prism_volume),
            (tet_volume_hbm, tet_volume),
            (face_lift_hbm, face_lift),
            (wall_lift_hbm, wall_lift),
            (law_hbm, law_ref),
        ),
        load_sem,
    )
    barrier = pltpu.get_barrier_semaphore()

    @pl.when(has_low)
    def _():
        pl.semaphore_signal(barrier, inc=1, device_id=low, device_id_type=mesh_id)

    @pl.when(has_high)
    def _():
        pl.semaphore_signal(barrier, inc=1, device_id=high, device_id_type=mesh_id)

    for other in others:
        pl.semaphore_signal(barrier, inc=1, device_id=other, device_id_type=mesh_id)

    prisms = prism_ref.shape[1]
    tets, slots = hot.shape
    half = slots // 2
    faces_spread = spread(FACES, face_extrap.shape[1] // FACES, FACE_PAD)
    wall_spread = spread(NV, TFP, VAR_PAD)

    def face_copy(side, device):
        return pltpu.make_async_remote_copy(
            src_ref=send.at[side],
            dst_ref=right_hbm.at[1 - side],
            send_sem=send_sem.at[side],
            recv_sem=recv_sem.at[1 - side],
            device_id=device,
            device_id_type=mesh_id,
        )

    loads[0].wait()
    extrap = dot_t(faces_spread, face_extrap[...]).astype(BF16)
    loads[1].wait()
    code = code_ref[...]
    tet_index = code // FACES
    face = code - FACES * tet_index
    for side in range(2):
        lanes = slice(side * half, (side + 1) * half)
        for base in range(0, tets, CHUNK):
            hot[base : base + CHUNK, lanes] = one_hot(tet_index[:, lanes], base, CHUNK)
        if side == 0:
            loads[2].wait()
        columns = dot(tet_ref[...], hot[:, lanes]).astype(BF16)
        extended = dot(extrap, columns)
        rows = extended[0:FACE_PAD]
        for f in range(1, FACES):
            rows = jnp.where(
                face[:, lanes] == f, extended[f * FACE_PAD : (f + 1) * FACE_PAD], rows
            )
        send[side] = rows.astype(BF16)
        if side == 0:

            @pl.when(has_low & has_high)
            def _():
                pl.semaphore_wait(barrier, n_azim + 1)

            @pl.when(jnp.logical_not(has_low & has_high))
            def _():
                pl.semaphore_wait(barrier, n_azim)

        @pl.when(has_high if side else has_low)
        def _():
            face_copy(side, high if side else low).start()

    for load in loads[3:7]:
        load.wait()
    wall_out = dot(wall_spread, wall_extrap[...]).astype(BF16)
    wall_rows = dot(wall_out, prism_ref[...]).astype(BF16).astype(F32)
    squares = wall_rows[(NV - 1) * VAR_PAD : NV * VAR_PAD]
    squares = squares * squares
    owner_row = lax.broadcasted_iota(jnp.int32, (OWNER_ROWS, owner_ref.shape[1]), 0)
    owner_hot = jnp.where(owner_row == owner_ref[...], 1.0, 0.0).astype(BF16)
    owned = dot_t(owner_hot, one_hot(burn_ref[...], 0, prisms))
    partial = jnp.sum(owned * jnp.sum(squares, axis=0, keepdims=True), axis=1, keepdims=True)
    part[...] = jnp.broadcast_to(partial, part.shape)

    def part_copy(source, d):
        return pltpu.make_async_remote_copy(
            src_ref=part,
            dst_ref=parts.at[source],
            send_sem=part_send_sem.at[d],
            recv_sem=part_recv_sem.at[source],
            device_id=others[d],
            device_id_type=mesh_id,
        )

    for d in range(n_azim - 1):
        part_copy(azim, d).start()

    for load in loads[7:]:
        load.wait()
    tet_state = tet_ref[...]
    tet_base[...] = tet_state.astype(F32) - section_step * dot(
        tet_volume[...], square_half(tet_state)
    )
    lift[...] = dot_t(face_lift[...], faces_spread).astype(BF16)
    stores = load_all(
        ((send, left_hbm), (tet_base, base_hbm), (lift, lift_hbm)), store_sem
    )
    wall_in = lax.dot_general(
        wall_lift[...], wall_spread, (((0,), (1,)), ((), ())), preferred_element_type=F32
    ).astype(BF16)
    for first in range(0, prisms, half):
        lanes = slice(first, first + half)
        state = prism_ref[:, lanes]
        prism_base[:, lanes] = state.astype(F32) - section_step * dot(
            prism_volume[...], square_half(state)
        )

    sums = part[...]
    for d in range(n_azim - 1):
        part_copy(azim, d).wait_send()
        source = others[d][1]
        part_copy(source, d).wait_recv()
        sums = sums + parts[source]
    faces = owner_ref.shape[1]
    inject = [jnp.zeros((1, prisms), F32) for _ in range(NV)]
    walls = jnp.zeros((1, prisms), F32)
    for o in range(n_azim):
        burn = law_ref[o : o + 1, 0:1]
        damping = 1.0 / (1.0 + burn * sums[o : o + 1, 0:1] / (faces * TFP))
        scale = owned[o : o + 1] * (burn * damping)
        walls = walls + owned[o : o + 1]
        for v in range(NV):
            inject[v] = inject[v] + law_ref[o : o + 1, 1 + v : 2 + v] * scale
    wall_jump = jnp.concatenate(
        [
            jnp.where(
                walls > 0.5,
                inject[v] * squares - wall_rows[v * VAR_PAD : (v + 1) * VAR_PAD],
                0.0,
            ).astype(BF16)
            for v in range(NV)
        ],
        axis=0,
    )
    for first in range(0, prisms, half):
        lanes = slice(first, first + half)
        lifted = dot(wall_in, wall_jump[:, lanes])
        prism_new[:, lanes] = (prism_base[:, lanes] - section_step * lifted).astype(BF16)
    last = pltpu.make_async_copy(prism_new, prism_new_hbm, store_sem.at[len(stores)])
    last.start()

    @pl.when(has_low)
    def _():
        face_copy(0, low).wait_send()
        face_copy(1, low).wait_recv()

    @pl.when(has_high)
    def _():
        face_copy(1, high).wait_send()
        face_copy(0, high).wait_recv()

    for store in stores:
        store.wait()
    last.wait()


def finish(
    code_hbm,
    count_hbm,
    area_hbm,
    left_hbm,
    right_hbm,
    base_hbm,
    lift_hbm,
    prism_new_hbm,
    tet_out,
    prism_out,
    code_ref,
    count_ref,
    area_ref,
    left_ref,
    right_ref,
    tet_base,
    lift,
    prism_new,
    tet_new,
    hot,
    load_sem,
    store_sem,
):
    loads = load_all(
        (
            (code_hbm, code_ref),
            (count_hbm, count_ref),
            (area_hbm, area_ref),
            (left_hbm, left_ref),
            (right_hbm, right_ref),
            (lift_hbm, lift),
            (prism_new_hbm, prism_new),
            (base_hbm, tet_base),
        ),
        load_sem,
    )
    tets, slots = hot.shape
    half = slots // 2
    loads[0].wait()
    code = code_ref[...]
    tet_index = code // FACES
    face = code - FACES * tet_index
    for base in range(0, tets, CHUNK):
        hot[base : base + CHUNK, :] = one_hot(tet_index, base, CHUNK)
    for load in loads[1:7]:
        load.wait()
    out_copy = pltpu.make_async_copy(prism_new, prism_out, store_sem.at[0])
    out_copy.start()

    slot = lax.broadcasted_iota(jnp.int32, (1, half), 1)
    jumps = []
    for side in range(2):
        lanes = slice(side * half, (side + 1) * half)
        left = left_ref[side].astype(F32)
        right = right_ref[side].astype(F32)
        speed = jnp.maximum(jnp.abs(left), jnp.abs(right))
        step = right - left
        normal = 0.25 if side else -0.25
        flux_jump = normal * (right * right - left * left) - 0.5 * speed * step
        live = slot < count_ref[0:1, side : side + 1]
        jumps.append(jnp.where(live, area_ref[:, lanes] * flux_jump, 0.0).astype(BF16))
    jump = jnp.concatenate(jumps, axis=1)
    zero = jnp.zeros_like(jump)
    placed = jnp.concatenate([jnp.where(face == f, jump, zero) for f in range(FACES)], axis=0)
    on_tets = dot_t(placed, hot[...]).astype(BF16)
    lifted = dot(lift[...], on_tets)
    loads[7].wait()
    tet_new[...] = (tet_base[...] - section_step * lifted).astype(BF16)
    last = pltpu.make_async_copy(tet_new, tet_out, store_sem.at[1])
    last.start()
    out_copy.wait()
    last.wait()


def on_device(
    n_axial,
    n_azim,
    tet_state,
    prism_state,
    tet_volume,
    prism_volume,
    face_extrap,
    face_lift,
    wall_extrap,
    wall_lift,
    face_code,
    face_count,
    face_area,
    burn_prism,
    burn_owner,
    burn_law,
):
    slots = face_code.shape[0]
    faces = burn_prism.shape[0]
    tets = tet_state.shape[1]
    hbm = pl.BlockSpec(memory_space=pltpu.HBM)
    dma = pltpu.SemaphoreType.DMA

    def vmem(arrays):
        return [pltpu.VMEM(x.shape, x.dtype) for x in arrays]

    code = face_code.reshape(1, slots)
    operands = (
        tet_state,
        prism_state,
        tet_volume,
        prism_volume,
        face_extrap.T,
        face_lift,
        wall_extrap,
        wall_lift.T,
        code,
        burn_prism.reshape(1, faces),
        burn_owner.reshape(1, faces),
        burn_law[0],
    )
    rows = jax.ShapeDtypeStruct((2, FACE_PAD, slots // 2), BF16)
    base = jax.ShapeDtypeStruct(tet_state.shape, F32)
    lift = jax.ShapeDtypeStruct((tet_state.shape[0], FACES * FACE_PAD), BF16)
    prism_new = jax.ShapeDtypeStruct(prism_state.shape, BF16)
    tet_new = jax.ShapeDtypeStruct(tet_state.shape, BF16)
    between = pl.pallas_call(
        functools.partial(exchange, n_axial, n_azim),
        out_shape=(rows, rows, base, lift, prism_new),
        in_specs=[hbm] * len(operands),
        out_specs=[hbm] * 5,
        scratch_shapes=vmem(operands)
        + vmem((rows, base, lift, prism_new))
        + [
            pltpu.VMEM((tets, slots), BF16),
            pltpu.VMEM(prism_state.shape, F32),
            pltpu.VMEM((OWNER_ROWS, 128), F32),
            pltpu.VMEM((n_azim, OWNER_ROWS, 128), F32),
            dma((len(operands),)),
            dma((4,)),
            dma((2,)),
            dma((2,)),
            dma((n_azim - 1,)),
            dma((n_azim,)),
        ],
        compiler_params=pltpu.CompilerParams(
            collective_id=0, has_side_effects=True, vmem_limit_bytes=VMEM_LIMIT
        ),
        name="exchange",
    )(*operands)
    inputs = (code, face_count, face_area.reshape(1, slots)) + tuple(between)
    return pl.pallas_call(
        finish,
        out_shape=(tet_new, prism_new),
        in_specs=[hbm] * len(inputs),
        out_specs=[hbm] * 2,
        scratch_shapes=vmem(inputs[:4])
        + vmem((rows, base, lift, prism_new, tet_new))
        + [pltpu.VMEM((tets, slots), BF16), dma((len(inputs),)), dma((2,))],
        compiler_params=pltpu.CompilerParams(vmem_limit_bytes=VMEM_LIMIT),
        name="finish",
    )(*inputs)


def solution(mesh):
    placed = (
        P(None, ("axial", "azim")),
        P(None, ("axial", "azim")),
        P(),
        P(),
        P(),
        P(),
        P(),
        P(),
        P(("axial", "azim")),
        P(("axial", "azim"), None),
        P(("axial", "azim")),
        P(("axial", "azim")),
        P(("axial", "azim"), None),
        P("axial", None, None),
    )
    return jax.shard_map(
        functools.partial(on_device, mesh.shape["axial"], mesh.shape["azim"]),
        mesh=mesh,
        in_specs=placed,
        out_specs=(P(None, ("axial", "azim")), P(None, ("axial", "azim"))),
        check_vma=False,
    )
```

```python
import functools

import jax
import jax.numpy as jnp
from jax import lax
from jax.experimental import pallas as pl
from jax.experimental.pallas import tpu as pltpu
from jax.sharding import PartitionSpec as P

NV = 5
TFP = 15
FACES = 4
FACE_PAD = 80
VAR_PAD = 16
OWNER_ROWS = 8
CHUNK = 256
VMEM_LIMIT = 63 * 1024 * 1024

section_step = 0.25
F32 = jnp.float32
BF16 = jnp.bfloat16


def dot(left, right):
    return jnp.dot(left, right, preferred_element_type=F32)


def dot_t(left, right):
    return lax.dot_general(left, right, (((1,), (1,)), ((), ())), preferred_element_type=F32)


def square_half(values):
    widened = values.astype(F32)
    return (0.5 * widened * widened).astype(BF16)


def spread(groups, width, padded):
    row = lax.broadcasted_iota(jnp.int32, (groups * padded, groups * width), 0)
    column = lax.broadcasted_iota(jnp.int32, (groups * padded, groups * width), 1)
    group = jnp.zeros_like(row)
    for g in range(1, groups):
        group = group + (row >= g * padded).astype(jnp.int32)
    hit = (column == row - group * (padded - width)) & (row - group * padded < width)
    return jnp.where(hit, 1.0, 0.0).astype(BF16)


def one_hot(index, base, rows):
    row = lax.broadcasted_iota(jnp.int32, (rows, index.shape[1]), 0) + base
    return jnp.where(row == index, 1.0, 0.0).astype(BF16)


def load_all(pairs, sem):
    loads = [
        pltpu.make_async_copy(source, target, sem.at[i])
        for i, (source, target) in enumerate(pairs)
    ]
    for load in loads:
        load.start()
    return loads


def exchange(
    n_axial,
    n_azim,
    tet_hbm,
    prism_hbm,
    tet_volume_hbm,
    prism_volume_hbm,
    face_extrap_hbm,
    face_lift_hbm,
    wall_extrap_hbm,
    wall_lift_hbm,
    code_hbm,
    burn_hbm,
    owner_hbm,
    left_hbm,
    right_hbm,
    tet_base_hbm,
    lift_hbm,
    parts_hbm,
    owned_hbm,
    wall_rows_hbm,
    wall_in_hbm,
    prism_base_hbm,
    tet_ref,
    prism_ref,
    tet_volume,
    prism_volume,
    face_extrap,
    face_lift,
    wall_extrap,
    wall_lift,
    code_ref,
    burn_ref,
    owner_ref,
    send,
    tet_base,
    lift,
    owned,
    wall_rows,
    wall_in,
    prism_base,
    hot,
    part,
    load_sem,
    store_sem,
    send_sem,
    recv_sem,
    part_send_sem,
    part_recv_sem,
):
    axial = lax.axis_index("axial")
    azim = lax.axis_index("azim")
    has_low = axial > 0
    has_high = axial < n_axial - 1
    low = (jnp.maximum(axial - 1, 0), azim)
    high = (jnp.minimum(axial + 1, n_axial - 1), azim)
    others = [(axial, lax.rem(azim + d, n_azim)) for d in range(1, n_azim)]
    mesh_id = pl.DeviceIdType.MESH

    loads = load_all(
        (
            (face_extrap_hbm, face_extrap),
            (code_hbm, code_ref),
            (tet_hbm, tet_ref),
            (burn_hbm, burn_ref),
            (owner_hbm, owner_ref),
            (wall_extrap_hbm, wall_extrap),
            (prism_hbm, prism_ref),
            (prism_volume_hbm, prism_volume),
            (tet_volume_hbm, tet_volume),
            (face_lift_hbm, face_lift),
            (wall_lift_hbm, wall_lift),
        ),
        load_sem,
    )
    barrier = pltpu.get_barrier_semaphore()

    @pl.when(has_low)
    def _():
        pl.semaphore_signal(barrier, inc=1, device_id=low, device_id_type=mesh_id)

    @pl.when(has_high)
    def _():
        pl.semaphore_signal(barrier, inc=1, device_id=high, device_id_type=mesh_id)

    for other in others:
        pl.semaphore_signal(barrier, inc=1, device_id=other, device_id_type=mesh_id)

    prisms = prism_ref.shape[1]
    tets, slots = hot.shape
    half = slots // 2
    faces_spread = spread(FACES, face_extrap.shape[1] // FACES, FACE_PAD)
    wall_spread = spread(NV, TFP, VAR_PAD)

    def face_copy(side, device):
        return pltpu.make_async_remote_copy(
            src_ref=send.at[side],
            dst_ref=right_hbm.at[1 - side],
            send_sem=send_sem.at[side],
            recv_sem=recv_sem.at[1 - side],
            device_id=device,
            device_id_type=mesh_id,
        )

    loads[0].wait()
    extrap = dot_t(faces_spread, face_extrap[...]).astype(BF16)
    loads[1].wait()
    code = code_ref[...]
    tet_index = code // FACES
    face = code - FACES * tet_index
    for side in range(2):
        lanes = slice(side * half, (side + 1) * half)
        for base in range(0, tets, CHUNK):
            hot[base : base + CHUNK, lanes] = one_hot(tet_index[:, lanes], base, CHUNK)
        if side == 0:
            loads[2].wait()
        columns = dot(tet_ref[...], hot[:, lanes]).astype(BF16)
        extended = dot(extrap, columns)
        rows = extended[0:FACE_PAD]
        for f in range(1, FACES):
            rows = jnp.where(
                face[:, lanes] == f, extended[f * FACE_PAD : (f + 1) * FACE_PAD], rows
            )
        send[side] = rows.astype(BF16)
        if side == 0:

            @pl.when(has_low & has_high)
            def _():
                pl.semaphore_wait(barrier, n_azim + 1)

            @pl.when(jnp.logical_not(has_low & has_high))
            def _():
                pl.semaphore_wait(barrier, n_azim)

        @pl.when(has_high if side else has_low)
        def _():
            face_copy(side, high if side else low).start()

    for load in loads[3:7]:
        load.wait()
    wall_out = dot(wall_spread, wall_extrap[...]).astype(BF16)
    wall_rows[...] = dot(wall_out, prism_ref[...]).astype(BF16)
    squares = wall_rows[(NV - 1) * VAR_PAD : NV * VAR_PAD, :].astype(F32)
    squares = squares * squares
    owner_row = lax.broadcasted_iota(jnp.int32, (OWNER_ROWS, owner_ref.shape[1]), 0)
    owner_hot = jnp.where(owner_row == owner_ref[...], 1.0, 0.0).astype(BF16)
    owned[...] = dot_t(owner_hot, one_hot(burn_ref[...], 0, prisms))
    partial = jnp.sum(owned[...] * jnp.sum(squares, axis=0, keepdims=True), axis=1, keepdims=True)
    part[...] = jnp.broadcast_to(partial, part.shape)

    def part_copy(source, d):
        return pltpu.make_async_remote_copy(
            src_ref=part,
            dst_ref=parts_hbm.at[source],
            send_sem=part_send_sem.at[d],
            recv_sem=part_recv_sem.at[source],
            device_id=others[d],
            device_id_type=mesh_id,
        )

    for d in range(n_azim - 1):
        part_copy(azim, d).start()

    for load in loads[7:]:
        load.wait()
    tet_state = tet_ref[...]
    tet_base[...] = tet_state.astype(F32) - section_step * dot(
        tet_volume[...], square_half(tet_state)
    )
    lift[...] = dot_t(face_lift[...], faces_spread).astype(BF16)
    wall_in[...] = lax.dot_general(
        wall_lift[...], wall_spread, (((0,), (1,)), ((), ())), preferred_element_type=F32
    ).astype(BF16)
    stores = load_all(
        (
            (part, parts_hbm.at[azim]),
            (send, left_hbm),
            (tet_base, tet_base_hbm),
            (lift, lift_hbm),
            (owned, owned_hbm),
            (wall_rows, wall_rows_hbm),
            (wall_in, wall_in_hbm),
        ),
        store_sem,
    )
    for first in range(0, prisms, half):
        lanes = slice(first, first + half)
        state = prism_ref[:, lanes]
        prism_base[:, lanes] = state.astype(F32) - section_step * dot(
            prism_volume[...], square_half(state)
        )
    last = pltpu.make_async_copy(prism_base, prism_base_hbm, store_sem.at[len(stores)])
    last.start()
    for d in range(n_azim - 1):
        part_copy(azim, d).wait_send()
        part_copy(others[d][1], d).wait_recv()

    @pl.when(has_low)
    def _():
        face_copy(0, low).wait_send()
        face_copy(1, low).wait_recv()

    @pl.when(has_high)
    def _():
        face_copy(1, high).wait_send()
        face_copy(0, high).wait_recv()

    for store in stores:
        store.wait()
    last.wait()


def finish(
    n_azim,
    faces,
    code_hbm,
    count_hbm,
    area_hbm,
    law_hbm,
    left_hbm,
    right_hbm,
    tet_base_hbm,
    lift_hbm,
    parts_hbm,
    owned_hbm,
    wall_rows_hbm,
    wall_in_hbm,
    prism_base_hbm,
    tet_out,
    prism_out,
    code_ref,
    count_ref,
    area_ref,
    law_ref,
    left_ref,
    right_ref,
    tet_base,
    lift,
    parts,
    owned,
    wall_rows,
    wall_in,
    prism_base,
    tet_new,
    prism_new,
    hot,
    load_sem,
    store_sem,
):
    loads = load_all(
        (
            (code_hbm, code_ref),
            (left_hbm, left_ref),
            (right_hbm, right_ref),
            (area_hbm, area_ref),
            (count_hbm, count_ref),
            (lift_hbm, lift),
            (parts_hbm, parts),
            (owned_hbm, owned),
            (wall_rows_hbm, wall_rows),
            (law_hbm, law_ref),
            (wall_in_hbm, wall_in),
            (tet_base_hbm, tet_base),
            (prism_base_hbm, prism_base),
        ),
        load_sem,
    )
    tets, slots = hot.shape
    prisms = prism_new.shape[1]
    half = slots // 2
    stores = []

    def store(new, out, first, width):
        lanes = pl.ds(first, width)
        copy = pltpu.make_async_copy(
            new.at[:, lanes], out.at[:, lanes], store_sem.at[len(stores)]
        )
        copy.start()
        stores.append(copy)

    loads[0].wait()
    code = code_ref[...]
    tet_index = code // FACES
    face = code - FACES * tet_index
    for base in range(0, tets, CHUNK):
        hot[base : base + CHUNK, :] = one_hot(tet_index, base, CHUNK)
    for load in loads[1:11]:
        load.wait()

    sums = parts[0]
    for source in range(1, n_azim):
        sums = sums + parts[source]
    squares = wall_rows[(NV - 1) * VAR_PAD : NV * VAR_PAD, :].astype(F32)
    squares = squares * squares
    inject = [jnp.zeros((1, prisms), F32) for _ in range(NV)]
    walls = jnp.zeros((1, prisms), F32)
    for o in range(n_azim):
        burn = law_ref[o : o + 1, 0:1]
        damping = 1.0 / (1.0 + burn * sums[o : o + 1, 0:1] / (faces * TFP))
        mine = owned[o : o + 1, :]
        scale = mine * (burn * damping)
        walls = walls + mine
        for v in range(NV):
            inject[v] = inject[v] + law_ref[o : o + 1, 1 + v : 2 + v] * scale
    wall_jump = jnp.concatenate(
        [
            jnp.where(
                walls > 0.5,
                inject[v] * squares
                - wall_rows[v * VAR_PAD : (v + 1) * VAR_PAD, :].astype(F32),
                0.0,
            ).astype(BF16)
            for v in range(NV)
        ],
        axis=0,
    )

    slot = lax.broadcasted_iota(jnp.int32, (1, half), 1)
    jumps = []
    for side in range(2):
        lanes = slice(side * half, (side + 1) * half)
        left = left_ref[side].astype(F32)
        right = right_ref[side].astype(F32)
        speed = jnp.maximum(jnp.abs(left), jnp.abs(right))
        step = right - left
        normal = 0.25 if side else -0.25
        flux_jump = normal * (right * right - left * left) - 0.5 * speed * step
        live = slot < count_ref[0:1, side : side + 1]
        jumps.append(jnp.where(live, area_ref[:, lanes] * flux_jump, 0.0).astype(BF16))
    jump = jnp.concatenate(jumps, axis=1)
    zero = jnp.zeros_like(jump)
    placed = jnp.concatenate([jnp.where(face == f, jump, zero) for f in range(FACES)], axis=0)
    lifted = dot(lift[...], placed).astype(BF16)
    loads[11].wait()
    loads[12].wait()
    for first in range(0, prisms, half):
        lanes = slice(first, first + half)
        total = prism_base[:, lanes] - section_step * dot(wall_in[...], wall_jump[:, lanes])
        prism_new[:, lanes] = total.astype(BF16)
        store(prism_new, prism_out, first, half)
    for first in range(0, tets, half):
        lanes = slice(first, first + half)
        total = tet_base[:, lanes] - section_step * dot_t(lifted, hot[lanes, :])
        tet_new[:, lanes] = total.astype(BF16)
        store(tet_new, tet_out, first, half)
    for copy in stores:
        copy.wait()


def on_device(
    n_axial,
    n_azim,
    tet_state,
    prism_state,
    tet_volume,
    prism_volume,
    face_extrap,
    face_lift,
    wall_extrap,
    wall_lift,
    face_code,
    face_count,
    face_area,
    burn_prism,
    burn_owner,
    burn_law,
):
    slots = face_code.shape[0]
    faces = burn_prism.shape[0]
    tets = tet_state.shape[1]
    hbm = pl.BlockSpec(memory_space=pltpu.HBM)
    dma = pltpu.SemaphoreType.DMA

    def vmem(arrays):
        return [pltpu.VMEM(x.shape, x.dtype) for x in arrays]

    code = face_code.reshape(1, slots)
    operands = (
        tet_state,
        prism_state,
        tet_volume,
        prism_volume,
        face_extrap.T,
        face_lift,
        wall_extrap,
        wall_lift.T,
        code,
        burn_prism.reshape(1, faces),
        burn_owner.reshape(1, faces),
    )
    rows = jax.ShapeDtypeStruct((2, FACE_PAD, slots // 2), BF16)
    base = jax.ShapeDtypeStruct(tet_state.shape, F32)
    lift = jax.ShapeDtypeStruct((tet_state.shape[0], FACES * FACE_PAD), BF16)
    prism_new = jax.ShapeDtypeStruct(prism_state.shape, BF16)
    tet_new = jax.ShapeDtypeStruct(tet_state.shape, BF16)
    between = (
        rows,
        rows,
        base,
        lift,
        jax.ShapeDtypeStruct((n_azim, OWNER_ROWS, 128), F32),
        jax.ShapeDtypeStruct((OWNER_ROWS, prism_state.shape[1]), F32),
        jax.ShapeDtypeStruct((NV * VAR_PAD, prism_state.shape[1]), BF16),
        jax.ShapeDtypeStruct((prism_state.shape[0], NV * VAR_PAD), BF16),
        jax.ShapeDtypeStruct(prism_state.shape, F32),
    )
    results = pl.pallas_call(
        functools.partial(exchange, n_axial, n_azim),
        out_shape=between,
        in_specs=[hbm] * len(operands),
        out_specs=[hbm] * len(between),
        scratch_shapes=vmem(operands)
        + vmem((rows, base, lift) + between[5:])
        + [
            pltpu.VMEM((tets, slots), BF16),
            pltpu.VMEM((OWNER_ROWS, 128), F32),
            dma((len(operands),)),
            dma((8,)),
            dma((2,)),
            dma((2,)),
            dma((n_azim - 1,)),
            dma((n_azim,)),
        ],
        compiler_params=pltpu.CompilerParams(
            collective_id=0, has_side_effects=True, vmem_limit_bytes=VMEM_LIMIT
        ),
        name="exchange",
    )(*operands)
    inputs = (code, face_count, face_area.reshape(1, slots), burn_law[0]) + tuple(results)
    return pl.pallas_call(
        functools.partial(finish, n_azim, faces),
        out_shape=(tet_new, prism_new),
        in_specs=[hbm] * len(inputs),
        out_specs=[hbm] * 2,
        scratch_shapes=vmem(inputs)
        + vmem((tet_new, prism_new))
        + [pltpu.VMEM((tets, slots), BF16), dma((len(inputs),)), dma((4,))],
        compiler_params=pltpu.CompilerParams(vmem_limit_bytes=VMEM_LIMIT),
        name="finish",
    )(*inputs)


def solution(mesh):
    placed = (
        P(None, ("axial", "azim")),
        P(None, ("axial", "azim")),
        P(),
        P(),
        P(),
        P(),
        P(),
        P(),
        P(("axial", "azim")),
        P(("axial", "azim"), None),
        P(("axial", "azim")),
        P(("axial", "azim")),
        P(("axial", "azim"), None),
        P("axial", None, None),
    )
    return jax.shard_map(
        functools.partial(on_device, mesh.shape["axial"], mesh.shape["azim"]),
        mesh=mesh,
        in_specs=placed,
        out_specs=(P(None, ("axial", "azim")), P(None, ("axial", "azim"))),
        check_vma=False,
    )
```

```python
import functools

import jax
import jax.numpy as jnp
from jax import lax
from jax.experimental import pallas as pl
from jax.experimental.pallas import tpu as pltpu
from jax.sharding import PartitionSpec as P

NV = 5
TFP = 15
FACES = 4
FACE_PAD = 80
VAR_PAD = 16
OWNER_ROWS = 8
CHUNK = 256
VMEM_LIMIT = 63 * 1024 * 1024

section_step = 0.25
F32 = jnp.float32
BF16 = jnp.bfloat16


def dot(left, right):
    return jnp.dot(left, right, preferred_element_type=F32)


def dot_t(left, right):
    return lax.dot_general(left, right, (((1,), (1,)), ((), ())), preferred_element_type=F32)


def square_half(values):
    widened = values.astype(F32)
    return (0.5 * widened * widened).astype(BF16)


def spread(groups, width, padded):
    row = lax.broadcasted_iota(jnp.int32, (groups * padded, groups * width), 0)
    column = lax.broadcasted_iota(jnp.int32, (groups * padded, groups * width), 1)
    group = jnp.zeros_like(row)
    for g in range(1, groups):
        group = group + (row >= g * padded).astype(jnp.int32)
    hit = (column == row - group * (padded - width)) & (row - group * padded < width)
    return jnp.where(hit, 1.0, 0.0).astype(BF16)


def one_hot(index, base, rows):
    row = lax.broadcasted_iota(jnp.int32, (rows, index.shape[1]), 0) + base
    return jnp.where(row == index, 1.0, 0.0).astype(BF16)


def load_all(pairs, sem):
    loads = [
        pltpu.make_async_copy(source, target, sem.at[i])
        for i, (source, target) in enumerate(pairs)
    ]
    for load in loads:
        load.start()
    return loads


def exchange(
    n_axial,
    n_azim,
    tet_hbm,
    prism_hbm,
    tet_volume_hbm,
    prism_volume_hbm,
    face_extrap_hbm,
    face_lift_hbm,
    wall_extrap_hbm,
    wall_lift_hbm,
    code_hbm,
    burn_hbm,
    owner_hbm,
    left_hbm,
    right_hbm,
    tet_base_hbm,
    lift_hbm,
    parts_hbm,
    owned_hbm,
    wall_rows_hbm,
    wall_in_hbm,
    prism_base_hbm,
    tet_ref,
    prism_ref,
    tet_volume,
    prism_volume,
    face_extrap,
    face_lift,
    wall_extrap,
    wall_lift,
    code_ref,
    burn_ref,
    owner_ref,
    send,
    tet_base,
    lift,
    owned,
    wall_rows,
    wall_in,
    prism_base,
    hot,
    part,
    load_sem,
    store_sem,
    send_sem,
    recv_sem,
    part_send_sem,
    part_recv_sem,
):
    axial = lax.axis_index("axial")
    azim = lax.axis_index("azim")
    has_low = axial > 0
    has_high = axial < n_axial - 1
    low = (jnp.maximum(axial - 1, 0), azim)
    high = (jnp.minimum(axial + 1, n_axial - 1), azim)
    others = [(axial, lax.rem(azim + d, n_azim)) for d in range(1, n_azim)]
    mesh_id = pl.DeviceIdType.MESH

    loads = load_all(
        (
            (code_hbm, code_ref),
            (face_extrap_hbm, face_extrap),
            (tet_hbm, tet_ref),
            (burn_hbm, burn_ref),
            (owner_hbm, owner_ref),
            (wall_extrap_hbm, wall_extrap),
            (prism_hbm, prism_ref),
            (prism_volume_hbm, prism_volume),
            (tet_volume_hbm, tet_volume),
            (face_lift_hbm, face_lift),
            (wall_lift_hbm, wall_lift),
        ),
        load_sem,
    )
    barrier = pltpu.get_barrier_semaphore()

    @pl.when(has_low)
    def _():
        pl.semaphore_signal(barrier, inc=1, device_id=low, device_id_type=mesh_id)

    @pl.when(has_high)
    def _():
        pl.semaphore_signal(barrier, inc=1, device_id=high, device_id_type=mesh_id)

    for other in others:
        pl.semaphore_signal(barrier, inc=1, device_id=other, device_id_type=mesh_id)

    prisms = prism_ref.shape[1]
    tets, slots = hot.shape
    half = slots // 2
    faces_spread = spread(FACES, face_extrap.shape[1] // FACES, FACE_PAD)
    wall_spread = spread(NV, TFP, VAR_PAD)

    pieces = half // CHUNK

    def face_copy(side, piece, device):
        return pltpu.make_async_remote_copy(
            src_ref=send.at[side, piece],
            dst_ref=right_hbm.at[1 - side, piece],
            send_sem=send_sem.at[side, piece],
            recv_sem=recv_sem.at[1 - side, piece],
            device_id=device,
            device_id_type=mesh_id,
        )

    loads[1].wait()
    extrap = dot_t(faces_spread, face_extrap[...]).astype(BF16)
    loads[0].wait()
    code = code_ref[...]
    tet_index = code // FACES
    face = code - FACES * tet_index

    def of_piece(values, piece):
        starts = [side * half + piece * CHUNK for side in range(2)]
        return jnp.concatenate([values[:, start : start + CHUNK] for start in starts], axis=1)

    for piece in range(pieces):
        lanes = slice(2 * piece * CHUNK, 2 * (piece + 1) * CHUNK)
        piece_index = of_piece(tet_index, piece)
        piece_face = of_piece(face, piece)
        for base in range(0, tets, CHUNK):
            hot[base : base + CHUNK, lanes] = one_hot(piece_index, base, CHUNK)
        if piece == 0:
            loads[2].wait()
        columns = dot(tet_ref[...], hot[:, lanes]).astype(BF16)
        extended = dot(extrap, columns)
        rows = extended[0:FACE_PAD]
        for f in range(1, FACES):
            rows = jnp.where(piece_face == f, extended[f * FACE_PAD : (f + 1) * FACE_PAD], rows)
        rows = rows.astype(BF16)
        for side in range(2):
            send[side, piece] = rows[:, side * CHUNK : (side + 1) * CHUNK]
        if piece == 0:

            @pl.when(has_low & has_high)
            def _():
                pl.semaphore_wait(barrier, n_azim + 1)

            @pl.when(jnp.logical_not(has_low & has_high))
            def _():
                pl.semaphore_wait(barrier, n_azim)

        @pl.when(has_low)
        def _():
            face_copy(0, piece, low).start()

        @pl.when(has_high)
        def _():
            face_copy(1, piece, high).start()

    for load in loads[3:7]:
        load.wait()
    wall_out = dot(wall_spread, wall_extrap[...]).astype(BF16)
    wall_rows[...] = dot(wall_out, prism_ref[...]).astype(BF16)
    squares = wall_rows[(NV - 1) * VAR_PAD : NV * VAR_PAD, :].astype(F32)
    squares = squares * squares
    owner_row = lax.broadcasted_iota(jnp.int32, (OWNER_ROWS, owner_ref.shape[1]), 0)
    owner_hot = jnp.where(owner_row == owner_ref[...], 1.0, 0.0).astype(BF16)
    owned[...] = dot_t(owner_hot, one_hot(burn_ref[...], 0, prisms))
    partial = jnp.sum(owned[...] * jnp.sum(squares, axis=0, keepdims=True), axis=1, keepdims=True)
    part[...] = jnp.broadcast_to(partial, part.shape)

    def part_copy(source, d):
        return pltpu.make_async_remote_copy(
            src_ref=part,
            dst_ref=parts_hbm.at[source],
            send_sem=part_send_sem.at[d],
            recv_sem=part_recv_sem.at[source],
            device_id=others[d],
            device_id_type=mesh_id,
        )

    for d in range(n_azim - 1):
        part_copy(azim, d).start()

    for load in loads[7:]:
        load.wait()
    tet_state = tet_ref[...]
    tet_base[...] = tet_state.astype(F32) - section_step * dot(
        tet_volume[...], square_half(tet_state)
    )
    lift[...] = dot_t(face_lift[...], faces_spread).astype(BF16)
    wall_in[...] = lax.dot_general(
        wall_lift[...], wall_spread, (((0,), (1,)), ((), ())), preferred_element_type=F32
    ).astype(BF16)
    stores = load_all(
        (
            (part, parts_hbm.at[azim]),
            (send, left_hbm),
            (tet_base, tet_base_hbm),
            (lift, lift_hbm),
            (owned, owned_hbm),
            (wall_rows, wall_rows_hbm),
            (wall_in, wall_in_hbm),
        ),
        store_sem,
    )
    for first in range(0, prisms, half):
        lanes = slice(first, first + half)
        state = prism_ref[:, lanes]
        prism_base[:, lanes] = state.astype(F32) - section_step * dot(
            prism_volume[...], square_half(state)
        )
    last = pltpu.make_async_copy(prism_base, prism_base_hbm, store_sem.at[len(stores)])
    last.start()
    for d in range(n_azim - 1):
        part_copy(azim, d).wait_send()
        part_copy(others[d][1], d).wait_recv()

    @pl.when(has_low)
    def _():
        for piece in range(pieces):
            face_copy(0, piece, low).wait_send()
            face_copy(1, piece, low).wait_recv()

    @pl.when(has_high)
    def _():
        for piece in range(pieces):
            face_copy(1, piece, high).wait_send()
            face_copy(0, piece, high).wait_recv()

    for store in stores:
        store.wait()
    last.wait()


def finish(
    n_azim,
    faces,
    code_hbm,
    count_hbm,
    area_hbm,
    law_hbm,
    left_hbm,
    right_hbm,
    tet_base_hbm,
    lift_hbm,
    parts_hbm,
    owned_hbm,
    wall_rows_hbm,
    wall_in_hbm,
    prism_base_hbm,
    tet_out,
    prism_out,
    code_ref,
    count_ref,
    area_ref,
    law_ref,
    left_ref,
    right_ref,
    tet_base,
    lift,
    parts,
    owned,
    wall_rows,
    wall_in,
    prism_base,
    tet_new,
    prism_new,
    hot,
    load_sem,
    store_sem,
):
    loads = load_all(
        (
            (code_hbm, code_ref),
            (left_hbm, left_ref),
            (right_hbm, right_ref),
            (area_hbm, area_ref),
            (count_hbm, count_ref),
            (lift_hbm, lift),
            (parts_hbm, parts),
            (owned_hbm, owned),
            (wall_rows_hbm, wall_rows),
            (law_hbm, law_ref),
            (wall_in_hbm, wall_in),
            (tet_base_hbm, tet_base),
            (prism_base_hbm, prism_base),
        ),
        load_sem,
    )
    tets, slots = hot.shape
    prisms = prism_new.shape[1]
    half = slots // 2
    stores = []

    def store(new, out, first, width):
        lanes = pl.ds(first, width)
        copy = pltpu.make_async_copy(
            new.at[:, lanes], out.at[:, lanes], store_sem.at[len(stores)]
        )
        copy.start()
        stores.append(copy)

    loads[0].wait()
    code = code_ref[...]
    tet_index = code // FACES
    face = code - FACES * tet_index
    for base in range(0, tets, CHUNK):
        hot[base : base + CHUNK, :] = one_hot(tet_index, base, CHUNK)
    for load in loads[1:6]:
        load.wait()

    slot = lax.broadcasted_iota(jnp.int32, (1, CHUNK), 1)
    jumps = []
    for side in range(2):
        for piece in range(half // CHUNK):
            first = side * half + piece * CHUNK
            left = left_ref[side, piece].astype(F32)
            right = right_ref[side, piece].astype(F32)
            speed = jnp.maximum(jnp.abs(left), jnp.abs(right))
            step = right - left
            normal = 0.25 if side else -0.25
            flux_jump = normal * (right * right - left * left) - 0.5 * speed * step
            live = slot + piece * CHUNK < count_ref[0:1, side : side + 1]
            area = area_ref[:, first : first + CHUNK]
            jumps.append(jnp.where(live, area * flux_jump, 0.0).astype(BF16))
    jump = jnp.concatenate(jumps, axis=1)
    zero = jnp.zeros_like(jump)
    placed = jnp.concatenate([jnp.where(face == f, jump, zero) for f in range(FACES)], axis=0)
    lifted = dot(lift[...], placed).astype(BF16)
    for load in loads[6:12]:
        load.wait()
    for first in range(0, tets, half):
        lanes = slice(first, first + half)
        total = tet_base[:, lanes] - section_step * dot_t(lifted, hot[lanes, :])
        tet_new[:, lanes] = total.astype(BF16)
        store(tet_new, tet_out, first, half)

    sums = parts[0]
    for source in range(1, n_azim):
        sums = sums + parts[source]
    squares = wall_rows[(NV - 1) * VAR_PAD : NV * VAR_PAD, :].astype(F32)
    squares = squares * squares
    inject = [jnp.zeros((1, prisms), F32) for _ in range(NV)]
    walls = jnp.zeros((1, prisms), F32)
    for o in range(n_azim):
        burn = law_ref[o : o + 1, 0:1]
        damping = 1.0 / (1.0 + burn * sums[o : o + 1, 0:1] / (faces * TFP))
        mine = owned[o : o + 1, :]
        scale = mine * (burn * damping)
        walls = walls + mine
        for v in range(NV):
            inject[v] = inject[v] + law_ref[o : o + 1, 1 + v : 2 + v] * scale
    wall_jump = jnp.concatenate(
        [
            jnp.where(
                walls > 0.5,
                inject[v] * squares
                - wall_rows[v * VAR_PAD : (v + 1) * VAR_PAD, :].astype(F32),
                0.0,
            ).astype(BF16)
            for v in range(NV)
        ],
        axis=0,
    )

    loads[12].wait()
    for first in range(0, prisms, half):
        lanes = slice(first, first + half)
        total = prism_base[:, lanes] - section_step * dot(wall_in[...], wall_jump[:, lanes])
        prism_new[:, lanes] = total.astype(BF16)
        store(prism_new, prism_out, first, half)
    for copy in stores:
        copy.wait()


def on_device(
    n_axial,
    n_azim,
    tet_state,
    prism_state,
    tet_volume,
    prism_volume,
    face_extrap,
    face_lift,
    wall_extrap,
    wall_lift,
    face_code,
    face_count,
    face_area,
    burn_prism,
    burn_owner,
    burn_law,
):
    slots = face_code.shape[0]
    faces = burn_prism.shape[0]
    tets = tet_state.shape[1]
    hbm = pl.BlockSpec(memory_space=pltpu.HBM)
    dma = pltpu.SemaphoreType.DMA

    def vmem(arrays):
        return [pltpu.VMEM(x.shape, x.dtype) for x in arrays]

    code = face_code.reshape(1, slots)
    operands = (
        tet_state,
        prism_state,
        tet_volume,
        prism_volume,
        face_extrap.T,
        face_lift,
        wall_extrap,
        wall_lift.T,
        code,
        burn_prism.reshape(1, faces),
        burn_owner.reshape(1, faces),
    )
    rows = jax.ShapeDtypeStruct((2, slots // 2 // CHUNK, FACE_PAD, CHUNK), BF16)
    base = jax.ShapeDtypeStruct(tet_state.shape, F32)
    lift = jax.ShapeDtypeStruct((tet_state.shape[0], FACES * FACE_PAD), BF16)
    prism_new = jax.ShapeDtypeStruct(prism_state.shape, BF16)
    tet_new = jax.ShapeDtypeStruct(tet_state.shape, BF16)
    between = (
        rows,
        rows,
        base,
        lift,
        jax.ShapeDtypeStruct((n_azim, OWNER_ROWS, 128), F32),
        jax.ShapeDtypeStruct((OWNER_ROWS, prism_state.shape[1]), F32),
        jax.ShapeDtypeStruct((NV * VAR_PAD, prism_state.shape[1]), BF16),
        jax.ShapeDtypeStruct((prism_state.shape[0], NV * VAR_PAD), BF16),
        jax.ShapeDtypeStruct(prism_state.shape, F32),
    )
    results = pl.pallas_call(
        functools.partial(exchange, n_axial, n_azim),
        out_shape=between,
        in_specs=[hbm] * len(operands),
        out_specs=[hbm] * len(between),
        scratch_shapes=vmem(operands)
        + vmem((rows, base, lift) + between[5:])
        + [
            pltpu.VMEM((tets, slots), BF16),
            pltpu.VMEM((OWNER_ROWS, 128), F32),
            dma((len(operands),)),
            dma((8,)),
            dma(rows.shape[:2]),
            dma(rows.shape[:2]),
            dma((n_azim - 1,)),
            dma((n_azim,)),
        ],
        compiler_params=pltpu.CompilerParams(
            collective_id=0, has_side_effects=True, vmem_limit_bytes=VMEM_LIMIT
        ),
        name="exchange",
    )(*operands)
    inputs = (code, face_count, face_area.reshape(1, slots), burn_law[0]) + tuple(results)
    return pl.pallas_call(
        functools.partial(finish, n_azim, faces),
        out_shape=(tet_new, prism_new),
        in_specs=[hbm] * len(inputs),
        out_specs=[hbm] * 2,
        scratch_shapes=vmem(inputs)
        + vmem((tet_new, prism_new))
        + [pltpu.VMEM((tets, slots), BF16), dma((len(inputs),)), dma((4,))],
        compiler_params=pltpu.CompilerParams(vmem_limit_bytes=VMEM_LIMIT),
        name="finish",
    )(*inputs)


def solution(mesh):
    placed = (
        P(None, ("axial", "azim")),
        P(None, ("axial", "azim")),
        P(),
        P(),
        P(),
        P(),
        P(),
        P(),
        P(("axial", "azim")),
        P(("axial", "azim"), None),
        P(("axial", "azim")),
        P(("axial", "azim")),
        P(("axial", "azim"), None),
        P("axial", None, None),
    )
    return jax.shard_map(
        functools.partial(on_device, mesh.shape["axial"], mesh.shape["azim"]),
        mesh=mesh,
        in_specs=placed,
        out_specs=(P(None, ("axial", "azim")), P(None, ("axial", "azim"))),
        check_vma=False,
    )
```

```python
import functools

import jax
import jax.numpy as jnp
from jax import lax
from jax.experimental import pallas as pl
from jax.experimental.pallas import tpu as pltpu
from jax.sharding import PartitionSpec as P

NV = 5
TFP = 15
FACES = 4
FACE_PAD = 80
VAR_PAD = 16
OWNER_ROWS = 8
CHUNK = 256
PIECE = 128
VMEM_LIMIT = 63 * 1024 * 1024

section_step = 0.25
F32 = jnp.float32
BF16 = jnp.bfloat16


def dot(left, right):
    return jnp.dot(left, right, preferred_element_type=F32)


def dot_t(left, right):
    return lax.dot_general(left, right, (((1,), (1,)), ((), ())), preferred_element_type=F32)


def square_half(values):
    widened = values.astype(F32)
    return (0.5 * widened * widened).astype(BF16)


def spread(groups, width, padded):
    row = lax.broadcasted_iota(jnp.int32, (groups * padded, groups * width), 0)
    column = lax.broadcasted_iota(jnp.int32, (groups * padded, groups * width), 1)
    group = jnp.zeros_like(row)
    for g in range(1, groups):
        group = group + (row >= g * padded).astype(jnp.int32)
    hit = (column == row - group * (padded - width)) & (row - group * padded < width)
    return jnp.where(hit, 1.0, 0.0).astype(BF16)


def one_hot(index, base, rows):
    row = lax.broadcasted_iota(jnp.int32, (rows, index.shape[1]), 0) + base
    return jnp.where(row == index, 1.0, 0.0).astype(BF16)


def load_all(pairs, sem):
    loads = [
        pltpu.make_async_copy(source, target, sem.at[i])
        for i, (source, target) in enumerate(pairs)
    ]
    for load in loads:
        load.start()
    return loads


def exchange(
    n_axial,
    n_azim,
    tet_hbm,
    prism_hbm,
    tet_volume_hbm,
    prism_volume_hbm,
    face_extrap_hbm,
    face_lift_hbm,
    wall_extrap_hbm,
    wall_lift_hbm,
    code_hbm,
    burn_hbm,
    owner_hbm,
    left_hbm,
    right_hbm,
    tet_base_hbm,
    lift_hbm,
    parts_hbm,
    owned_hbm,
    wall_rows_hbm,
    wall_in_hbm,
    prism_base_hbm,
    tet_ref,
    prism_ref,
    tet_volume,
    prism_volume,
    face_extrap,
    face_lift,
    wall_extrap,
    wall_lift,
    code_ref,
    burn_ref,
    owner_ref,
    send,
    tet_base,
    lift,
    owned,
    wall_rows,
    wall_in,
    prism_base,
    hot,
    part,
    load_sem,
    store_sem,
    send_sem,
    recv_sem,
    part_send_sem,
    part_recv_sem,
):
    axial = lax.axis_index("axial")
    azim = lax.axis_index("azim")
    has_low = axial > 0
    has_high = axial < n_axial - 1
    low = (jnp.maximum(axial - 1, 0), azim)
    high = (jnp.minimum(axial + 1, n_axial - 1), azim)
    others = [(axial, lax.rem(azim + d, n_azim)) for d in range(1, n_azim)]
    mesh_id = pl.DeviceIdType.MESH

    loads = load_all(
        (
            (code_hbm, code_ref),
            (face_extrap_hbm, face_extrap),
            (tet_hbm, tet_ref),
            (burn_hbm, burn_ref),
            (owner_hbm, owner_ref),
            (wall_extrap_hbm, wall_extrap),
            (prism_hbm, prism_ref),
            (prism_volume_hbm, prism_volume),
            (tet_volume_hbm, tet_volume),
            (face_lift_hbm, face_lift),
            (wall_lift_hbm, wall_lift),
        ),
        load_sem,
    )
    barrier = pltpu.get_barrier_semaphore()

    @pl.when(has_low)
    def _():
        pl.semaphore_signal(barrier, inc=1, device_id=low, device_id_type=mesh_id)

    @pl.when(has_high)
    def _():
        pl.semaphore_signal(barrier, inc=1, device_id=high, device_id_type=mesh_id)

    for other in others:
        pl.semaphore_signal(barrier, inc=1, device_id=other, device_id_type=mesh_id)

    prisms = prism_ref.shape[1]
    tets, slots = hot.shape
    half = slots // 2
    faces_spread = spread(FACES, face_extrap.shape[1] // FACES, FACE_PAD)
    wall_spread = spread(NV, TFP, VAR_PAD)

    pieces = half // PIECE

    def face_copy(side, piece, device):
        return pltpu.make_async_remote_copy(
            src_ref=send.at[side, piece],
            dst_ref=right_hbm.at[1 - side, piece],
            send_sem=send_sem.at[side, piece],
            recv_sem=recv_sem.at[1 - side, piece],
            device_id=device,
            device_id_type=mesh_id,
        )

    loads[1].wait()
    extrap = dot_t(faces_spread, face_extrap[...]).astype(BF16)
    loads[0].wait()
    code = code_ref[...]
    tet_index = code // FACES
    face = code - FACES * tet_index

    def of_piece(values, piece):
        starts = [side * half + piece * PIECE for side in range(2)]
        return jnp.concatenate([values[:, start : start + PIECE] for start in starts], axis=1)

    for piece in range(pieces):
        lanes = slice(2 * piece * PIECE, 2 * (piece + 1) * PIECE)
        piece_index = of_piece(tet_index, piece)
        piece_face = of_piece(face, piece)
        for base in range(0, tets, CHUNK):
            hot[base : base + CHUNK, lanes] = one_hot(piece_index, base, CHUNK)
        if piece == 0:
            loads[2].wait()
        columns = dot(tet_ref[...], hot[:, lanes]).astype(BF16)
        extended = dot(extrap, columns)
        rows = extended[0:FACE_PAD]
        for f in range(1, FACES):
            rows = jnp.where(piece_face == f, extended[f * FACE_PAD : (f + 1) * FACE_PAD], rows)
        rows = rows.astype(BF16)
        for side in range(2):
            send[side, piece] = rows[:, side * PIECE : (side + 1) * PIECE]
        if piece == 0:

            @pl.when(has_low & has_high)
            def _():
                pl.semaphore_wait(barrier, n_azim + 1)

            @pl.when(jnp.logical_not(has_low & has_high))
            def _():
                pl.semaphore_wait(barrier, n_azim)

        @pl.when(has_low)
        def _():
            face_copy(0, piece, low).start()

        @pl.when(has_high)
        def _():
            face_copy(1, piece, high).start()

    for load in loads[3:7]:
        load.wait()
    wall_out = dot(wall_spread, wall_extrap[...]).astype(BF16)
    wall_rows[...] = dot(wall_out, prism_ref[...]).astype(BF16)
    squares = wall_rows[(NV - 1) * VAR_PAD : NV * VAR_PAD, :].astype(F32)
    squares = squares * squares
    owner_row = lax.broadcasted_iota(jnp.int32, (OWNER_ROWS, owner_ref.shape[1]), 0)
    owner_hot = jnp.where(owner_row == owner_ref[...], 1.0, 0.0).astype(BF16)
    owned[...] = dot_t(owner_hot, one_hot(burn_ref[...], 0, prisms))
    partial = jnp.sum(owned[...] * jnp.sum(squares, axis=0, keepdims=True), axis=1, keepdims=True)
    part[...] = jnp.broadcast_to(partial, part.shape)

    def part_copy(source, d):
        return pltpu.make_async_remote_copy(
            src_ref=part,
            dst_ref=parts_hbm.at[source],
            send_sem=part_send_sem.at[d],
            recv_sem=part_recv_sem.at[source],
            device_id=others[d],
            device_id_type=mesh_id,
        )

    for d in range(n_azim - 1):
        part_copy(azim, d).start()

    for load in loads[7:]:
        load.wait()
    tet_state = tet_ref[...]
    tet_base[...] = tet_state.astype(F32) - section_step * dot(
        tet_volume[...], square_half(tet_state)
    )
    lift[...] = dot_t(face_lift[...], faces_spread).astype(BF16)
    wall_in[...] = lax.dot_general(
        wall_lift[...], wall_spread, (((0,), (1,)), ((), ())), preferred_element_type=F32
    ).astype(BF16)
    stores = load_all(
        (
            (part, parts_hbm.at[azim]),
            (send, left_hbm),
            (tet_base, tet_base_hbm),
            (lift, lift_hbm),
            (owned, owned_hbm),
            (wall_rows, wall_rows_hbm),
            (wall_in, wall_in_hbm),
        ),
        store_sem,
    )
    for first in range(0, prisms, half):
        lanes = slice(first, first + half)
        state = prism_ref[:, lanes]
        prism_base[:, lanes] = state.astype(F32) - section_step * dot(
            prism_volume[...], square_half(state)
        )
        there = pl.ds(first, half)
        copy = pltpu.make_async_copy(
            prism_base.at[:, there], prism_base_hbm.at[:, there], store_sem.at[len(stores)]
        )
        copy.start()
        stores.append(copy)
    for d in range(n_azim - 1):
        part_copy(azim, d).wait_send()
        part_copy(others[d][1], d).wait_recv()

    @pl.when(has_low)
    def _():
        for piece in range(pieces):
            face_copy(0, piece, low).wait_send()
            face_copy(1, piece, low).wait_recv()

    @pl.when(has_high)
    def _():
        for piece in range(pieces):
            face_copy(1, piece, high).wait_send()
            face_copy(0, piece, high).wait_recv()

    for store in stores:
        store.wait()


def finish(
    n_azim,
    faces,
    code_hbm,
    count_hbm,
    area_hbm,
    law_hbm,
    left_hbm,
    right_hbm,
    tet_base_hbm,
    lift_hbm,
    parts_hbm,
    owned_hbm,
    wall_rows_hbm,
    wall_in_hbm,
    prism_base_hbm,
    tet_out,
    prism_out,
    code_ref,
    count_ref,
    area_ref,
    law_ref,
    left_ref,
    right_ref,
    tet_base,
    lift,
    parts,
    owned,
    wall_rows,
    wall_in,
    prism_base,
    tet_new,
    prism_new,
    hot,
    load_sem,
    store_sem,
):
    loads = load_all(
        (
            (code_hbm, code_ref),
            (left_hbm, left_ref),
            (right_hbm, right_ref),
            (area_hbm, area_ref),
            (count_hbm, count_ref),
            (lift_hbm, lift),
            (parts_hbm, parts),
            (owned_hbm, owned),
            (wall_rows_hbm, wall_rows),
            (law_hbm, law_ref),
            (wall_in_hbm, wall_in),
            (tet_base_hbm, tet_base),
            (prism_base_hbm, prism_base),
        ),
        load_sem,
    )
    tets, slots = hot.shape
    prisms = prism_new.shape[1]
    half = slots // 2
    stores = []

    def store(new, out, first, width):
        lanes = pl.ds(first, width)
        copy = pltpu.make_async_copy(
            new.at[:, lanes], out.at[:, lanes], store_sem.at[len(stores)]
        )
        copy.start()
        stores.append(copy)

    loads[0].wait()
    code = code_ref[...]
    tet_index = code // FACES
    face = code - FACES * tet_index
    for base in range(0, tets, CHUNK):
        hot[base : base + CHUNK, :] = one_hot(tet_index, base, CHUNK)
    for load in loads[1:6]:
        load.wait()

    slot = lax.broadcasted_iota(jnp.int32, (1, PIECE), 1)
    jumps = []
    for side in range(2):
        for piece in range(half // PIECE):
            first = side * half + piece * PIECE
            left = left_ref[side, piece].astype(F32)
            right = right_ref[side, piece].astype(F32)
            speed = jnp.maximum(jnp.abs(left), jnp.abs(right))
            step = right - left
            normal = 0.25 if side else -0.25
            flux_jump = normal * (right * right - left * left) - 0.5 * speed * step
            live = slot + piece * PIECE < count_ref[0:1, side : side + 1]
            area = area_ref[:, first : first + PIECE]
            jumps.append(jnp.where(live, area * flux_jump, 0.0).astype(BF16))
    jump = jnp.concatenate(jumps, axis=1)
    zero = jnp.zeros_like(jump)
    placed = jnp.concatenate([jnp.where(face == f, jump, zero) for f in range(FACES)], axis=0)
    lifted = dot(lift[...], placed).astype(BF16)
    for load in loads[6:12]:
        load.wait()
    for first in range(0, tets, half):
        lanes = slice(first, first + half)
        total = tet_base[:, lanes] - section_step * dot_t(lifted, hot[lanes, :])
        tet_new[:, lanes] = total.astype(BF16)
        store(tet_new, tet_out, first, half)

    sums = parts[0]
    for source in range(1, n_azim):
        sums = sums + parts[source]
    squares = wall_rows[(NV - 1) * VAR_PAD : NV * VAR_PAD, :].astype(F32)
    squares = squares * squares
    inject = [jnp.zeros((1, prisms), F32) for _ in range(NV)]
    walls = jnp.zeros((1, prisms), F32)
    for o in range(n_azim):
        burn = law_ref[o : o + 1, 0:1]
        damping = 1.0 / (1.0 + burn * sums[o : o + 1, 0:1] / (faces * TFP))
        mine = owned[o : o + 1, :]
        scale = mine * (burn * damping)
        walls = walls + mine
        for v in range(NV):
            inject[v] = inject[v] + law_ref[o : o + 1, 1 + v : 2 + v] * scale
    wall_jump = jnp.concatenate(
        [
            jnp.where(
                walls > 0.5,
                inject[v] * squares
                - wall_rows[v * VAR_PAD : (v + 1) * VAR_PAD, :].astype(F32),
                0.0,
            ).astype(BF16)
            for v in range(NV)
        ],
        axis=0,
    )

    loads[12].wait()
    for first in range(0, prisms, half):
        lanes = slice(first, first + half)
        total = prism_base[:, lanes] - section_step * dot(wall_in[...], wall_jump[:, lanes])
        prism_new[:, lanes] = total.astype(BF16)
        store(prism_new, prism_out, first, half)
    for copy in stores:
        copy.wait()


def on_device(
    n_axial,
    n_azim,
    tet_state,
    prism_state,
    tet_volume,
    prism_volume,
    face_extrap,
    face_lift,
    wall_extrap,
    wall_lift,
    face_code,
    face_count,
    face_area,
    burn_prism,
    burn_owner,
    burn_law,
):
    slots = face_code.shape[0]
    faces = burn_prism.shape[0]
    tets = tet_state.shape[1]
    hbm = pl.BlockSpec(memory_space=pltpu.HBM)
    dma = pltpu.SemaphoreType.DMA

    def vmem(arrays):
        return [pltpu.VMEM(x.shape, x.dtype) for x in arrays]

    code = face_code.reshape(1, slots)
    operands = (
        tet_state,
        prism_state,
        tet_volume,
        prism_volume,
        face_extrap.T,
        face_lift,
        wall_extrap,
        wall_lift.T,
        code,
        burn_prism.reshape(1, faces),
        burn_owner.reshape(1, faces),
    )
    rows = jax.ShapeDtypeStruct((2, slots // 2 // PIECE, FACE_PAD, PIECE), BF16)
    base = jax.ShapeDtypeStruct(tet_state.shape, F32)
    lift = jax.ShapeDtypeStruct((tet_state.shape[0], FACES * FACE_PAD), BF16)
    prism_new = jax.ShapeDtypeStruct(prism_state.shape, BF16)
    tet_new = jax.ShapeDtypeStruct(tet_state.shape, BF16)
    between = (
        rows,
        rows,
        base,
        lift,
        jax.ShapeDtypeStruct((n_azim, OWNER_ROWS, 128), F32),
        jax.ShapeDtypeStruct((OWNER_ROWS, prism_state.shape[1]), F32),
        jax.ShapeDtypeStruct((NV * VAR_PAD, prism_state.shape[1]), BF16),
        jax.ShapeDtypeStruct((prism_state.shape[0], NV * VAR_PAD), BF16),
        jax.ShapeDtypeStruct(prism_state.shape, F32),
    )
    results = pl.pallas_call(
        functools.partial(exchange, n_axial, n_azim),
        out_shape=between,
        in_specs=[hbm] * len(operands),
        out_specs=[hbm] * len(between),
        scratch_shapes=vmem(operands)
        + vmem((rows, base, lift) + between[5:])
        + [
            pltpu.VMEM((tets, slots), BF16),
            pltpu.VMEM((OWNER_ROWS, 128), F32),
            dma((len(operands),)),
            dma((9,)),
            dma(rows.shape[:2]),
            dma(rows.shape[:2]),
            dma((n_azim - 1,)),
            dma((n_azim,)),
        ],
        compiler_params=pltpu.CompilerParams(
            collective_id=0, has_side_effects=True, vmem_limit_bytes=VMEM_LIMIT
        ),
        name="exchange",
    )(*operands)
    inputs = (code, face_count, face_area.reshape(1, slots), burn_law[0]) + tuple(results)
    return pl.pallas_call(
        functools.partial(finish, n_azim, faces),
        out_shape=(tet_new, prism_new),
        in_specs=[hbm] * len(inputs),
        out_specs=[hbm] * 2,
        scratch_shapes=vmem(inputs)
        + vmem((tet_new, prism_new))
        + [pltpu.VMEM((tets, slots), BF16), dma((len(inputs),)), dma((4,))],
        compiler_params=pltpu.CompilerParams(vmem_limit_bytes=VMEM_LIMIT),
        name="finish",
    )(*inputs)


def solution(mesh):
    placed = (
        P(None, ("axial", "azim")),
        P(None, ("axial", "azim")),
        P(),
        P(),
        P(),
        P(),
        P(),
        P(),
        P(("axial", "azim")),
        P(("axial", "azim"), None),
        P(("axial", "azim")),
        P(("axial", "azim")),
        P(("axial", "azim"), None),
        P("axial", None, None),
    )
    return jax.shard_map(
        functools.partial(on_device, mesh.shape["axial"], mesh.shape["azim"]),
        mesh=mesh,
        in_specs=placed,
        out_specs=(P(None, ("axial", "azim")), P(None, ("axial", "azim"))),
        check_vma=False,
    )
```
